32 devices in a mesh: ctx: 8 (over z, x), head: 4 (over y, core).
Axes of the slice: x: 2, y: 2, z: 4, core: 2. Of those that a mesh axis runs over, the one named last changes fastest.
Arguments:
- query: bfloat16 [2048, 8192], P('ctx', 'head'), may hold values from -6 to 6
- keyval: bfloat16 [2048, 2048], P('ctx'), may hold values from -6 to 6
- grad_out: bfloat16 [2048, 8192], P('ctx', 'head'), may hold values from -6 to 6
- vis_blocks: int32 [16, 12], replicated, may hold values from 0 to 15, as said below
- vis_count: int32 [16], replicated, may hold values from 1 to 12, as said below
- segment_ids: int32 [2048], replicated, may hold values from 0 to 15, never falling along the last dimension, each value on 1 to 256 neighbouring positions
- block_order: int32 [16], replicated, may hold values from 0 to 15, as said below
Outputs:
- attn_out: bfloat16 [2048, 8192], P('ctx', 'head')
- grad_query: bfloat16 [2048, 8192], P('ctx', 'head')
- grad_keyval: float32 [2048, 2048], P('ctx')
The draws below stay inside these ranges and needn't reach their ends.
Inputs may be any that keep to these rules, and one draw needn't show every extreme that they name: `vis_blocks`: row b lists in rising order the blocks that block b's queries may see (block 0 and b itself always among them), then repeats b up to 12 entries. `vis_count`: the number of listed blocks of each row; some row lists exactly 12. `block_order`: storage blocks 2 i and 2 i + 1 hold visibility blocks p and 15 - p for some p; every block is held once. `segment_ids`: segment numbers never fall along the tokens in visibility-block order.
All inputs are finite; a program needn't handle non-finite values.
Results may differ from the reference program's by a relative error of at most 0.025.
Values may be sent and summed in bfloat16 or wider, within the bound.
A program may use at most 128 MiB of HBM per device.

```python
import math
import jax
import jax.numpy as jnp
import numpy as np
from jax import lax

QH = 64
KVH = 8
HD = 128
BLK = 128
NB = 16
MAXVIS = 12
TOKENS = 2048


def pair_order(key):
    pair_total = NB // 2
    picked = jax.random.permutation(jax.random.fold_in(key, 11), pair_total).astype(jnp.int32)
    flip_bits = jax.random.randint(jax.random.fold_in(key, 12), (pair_total,), 0, 2)
    first_ids = jnp.where(flip_bits == 1, NB - 1 - picked, picked)
    return jnp.stack([first_ids, NB - 1 - first_ids], axis=1).reshape(NB).astype(jnp.int32)


def visibility(key):
    shared = jax.random.randint(jax.random.fold_in(key, 21), (), NB // 8, NB // 2 + 1)
    prompt = jax.random.randint(jax.random.fold_in(key, 22), (), 1, shared)
    long_len = MAXVIS - shared
    short_len = NB - MAXVIS
    chosen_long = jax.random.randint(jax.random.fold_in(key, 23), (), 0, 2)
    chosen_len = jnp.where(chosen_long == 1, long_len, short_len)
    coin_bits = jax.random.randint(jax.random.fold_in(key, 24), (NB, NB), 0, 2)
    row_ids = jnp.arange(NB, dtype=jnp.int32)[:, None]
    col_ids = jnp.arange(NB, dtype=jnp.int32)[None, :]
    causal = col_ids <= row_ids
    in_prompt = row_ids < prompt
    in_tool = (row_ids >= prompt) & (row_ids < shared)
    in_chosen = (row_ids >= shared) & (row_ids < shared + chosen_len)
    in_rejected = row_ids >= shared + chosen_len
    tool_seen = (col_ids < prompt) | (col_ids == row_ids) | (col_ids >= prompt) & (coin_bits == 1)
    rejected_seen = (col_ids < shared) | (col_ids >= shared + chosen_len)
    seen = causal & (in_prompt | in_tool & tool_seen | in_chosen | in_rejected & rejected_seen)
    counts = jnp.sum(seen.astype(jnp.int32), axis=1).astype(jnp.int32)
    order_key = jnp.where(seen, col_ids, NB + col_ids)
    ranked = jnp.argsort(order_key, axis=1)[:, :MAXVIS].astype(jnp.int32)
    slot_ids = jnp.arange(MAXVIS, dtype=jnp.int32)[None, :]
    listed = jnp.where(slot_ids < counts[:, None], ranked, row_ids).astype(jnp.int32)
    return (listed, counts)


def draw_block_order(key, part):
    return pair_order(key)


def draw_vis_blocks(key, part):
    return visibility(key)[0]


def draw_vis_count(key, part):
    return visibility(key)[1]


def draw_query(key, part):
    own_key = jax.random.fold_in(key, 41)
    drawn = jnp.clip(jax.random.normal(jax.random.fold_in(own_key, 1), (TOKENS, QH * HD), jnp.float32), -6.0, 6.0)
    return drawn.astype(jnp.bfloat16)


def draw_keyval(key, part):
    own_key = jax.random.fold_in(key, 51)
    width_all = KVH * 2 * HD
    drawn = jnp.clip(jax.random.normal(jax.random.fold_in(own_key, 1), (TOKENS, width_all), jnp.float32), -6.0, 6.0)
    return drawn.astype(jnp.bfloat16)


def steps_of(rng, shape, shards, least, high):
    def one(position, shards_of):
        draws = jax.random.uniform(jax.random.fold_in(jax.random.fold_in(rng, 6), position), (shards_of,), jnp.float32, least / len(shards), high / len(shards))
        return jnp.repeat(jnp.exp(draws), shape[position] // shards_of).reshape((-1,) + (1,) * (len(shape) - position - 1))

    level = one(*shards[0])
    for cut in shards[1:]:
        level = level * one(*cut)
    return level


def split_up(amount, total, limit, slope):
    weights = [(1 << 20) // math.isqrt(rank ** slope) + 1 for rank in range(2, amount + 1)]
    surplus, holding = total - limit - (amount - 1), [1] * (amount - 1)
    while surplus > 0:
        candidates = [i for i in range(amount - 1) if holding[i] < limit]
        mass, remaining = sum([weights[i] for i in candidates]), surplus
        for i in candidates:
            addition = min(limit - holding[i], max(1, remaining * weights[i] // mass), surplus)
            holding[i] = holding[i] + addition
            surplus = surplus - addition
    return np.array([limit] + holding)


def ragged_sizes(rng, number_of, total, reach, slope):
    if number_of == 2:
        one = jax.random.randint(rng, (), max(1, total - reach), min(reach, total - 1) + 1)
        return jnp.stack([one, total - one])
    sizes = jnp.asarray(split_up(number_of, total, reach, slope), jnp.int32)
    couples = (number_of - 1) // 2
    donor, sink = sizes[1:1 + 2 * couples:2], sizes[2:2 + 2 * couples:2]
    margin = jnp.minimum(donor - 1, reach - sink)
    passed = jax.random.randint(jax.random.fold_in(rng, 1), (couples,), 0, 1 << 20) % (margin + 1)
    sizes = sizes.at[1:1 + 2 * couples:2].set(donor - passed).at[2:2 + 2 * couples:2].set(sink + passed)
    return sizes[jax.random.permutation(jax.random.fold_in(rng, 2), number_of)]


def bell_draw(key, shape, scale, limit, cuts=(), kind=jnp.bfloat16):
    array = scale * jax.random.normal(key, shape, jnp.float32)
    if cuts:
        array = array * steps_of(key, shape, cuts, -0.22, 0.18)
    return jnp.clip(array, -limit, limit).astype(kind)


def setup_inputs(seed: int = 0) -> dict:
    streams_of = jax.random.split(jax.random.key(seed), 8)
    return {
        "query": draw_query(jax.random.fold_in(streams_of[7], 71), 0),
        "keyval": draw_keyval(jax.random.fold_in(streams_of[7], 71), 0),
        "grad_out": bell_draw(streams_of[2], (TOKENS, QH * HD), 1.0, 6.0, ((0, 8), (1, 4))),
        "vis_blocks": draw_vis_blocks(jax.random.fold_in(streams_of[7], 71), 0),
        "vis_count": draw_vis_count(jax.random.fold_in(streams_of[7], 71), 0),
        "segment_ids": jnp.searchsorted(jnp.cumsum(ragged_sizes(streams_of[5], NB, TOKENS, 2 * BLK, 2)), jnp.arange(TOKENS), side="right").astype(jnp.int32),
        "block_order": draw_block_order(jax.random.fold_in(streams_of[7], 71), 0),
    }


very_negative = -1.0e30


def reference(query, keyval, grad_out, vis_blocks, vis_count, segment_ids, block_order):
    group_size = QH // KVH
    score_scale = HD ** -0.5
    highest = lax.Precision.HIGHEST
    positions = jnp.arange(NB, dtype=jnp.int32)
    inverse = jnp.sum(jnp.where(block_order[None, :] == positions[:, None], positions[None, :], 0), axis=1).astype(jnp.int32)
    query_pack = query.reshape(NB, BLK, KVH, group_size, HD)[inverse]
    keyval_pack = keyval.reshape(NB, BLK, KVH, 2, HD)[inverse]
    grad_pack = grad_out.reshape(NB, BLK, KVH, group_size, HD)[inverse]
    segment_pack = segment_ids.reshape(NB, BLK)
    token_pos = jnp.arange(BLK, dtype=jnp.int32)
    lower_part = token_pos[None, :] <= token_pos[:, None]
    slot_pos = jnp.arange(MAXVIS, dtype=jnp.int32)

    def one_block(dkv_acc, block_id):
        listed = vis_blocks[block_id]
        count_here = vis_count[block_id]
        q_here = query_pack[block_id].astype(jnp.float32)
        g_here = grad_pack[block_id].astype(jnp.float32)
        seg_here = segment_pack[block_id]
        intra = lower_part & (seg_here[:, None] == seg_here[None, :])
        valid = slot_pos < count_here
        own_slot = listed == block_id
        seen = valid[:, None, None] & (jnp.logical_not(own_slot)[:, None, None] | intra[None, :, :])
        seen = jnp.transpose(seen, (1, 0, 2))[None, None]
        fetched = keyval_pack[listed].astype(jnp.float32)
        key_part = fetched[:, :, :, 0, :]
        value_part = fetched[:, :, :, 1, :]
        scores = jnp.einsum("qhgd,mkhd->hgqmk", q_here, key_part, precision=highest) * score_scale
        row_max = jnp.max(jnp.where(seen, scores, very_negative), axis=(3, 4), keepdims=True)
        row_sum = jnp.sum(jnp.where(seen, jnp.exp(scores - row_max), 0.0), axis=(3, 4), keepdims=True)
        log_total = row_max + jnp.log(row_sum)
        weights = jnp.where(seen, jnp.exp(scores - log_total), 0.0)
        weights_low = lax.optimization_barrier(weights.astype(jnp.bfloat16)).astype(jnp.float32)
        out_here = jnp.einsum("hgqmk,mkhd->qhgd", weights_low, value_part, precision=highest).astype(jnp.bfloat16)
        out_wide = lax.optimization_barrier(out_here).astype(jnp.float32)
        delta = jnp.einsum("qhgd,qhgd->hgq", g_here, out_wide, precision=highest)
        grad_weights = jnp.einsum("qhgd,mkhd->hgqmk", g_here, value_part, precision=highest)
        grad_scores = (weights * (grad_weights - delta[:, :, :, None, None])).astype(jnp.bfloat16)
        grad_low = lax.optimization_barrier(grad_scores).astype(jnp.float32)
        dq_here = (jnp.einsum("hgqmk,mkhd->qhgd", grad_low, key_part, precision=highest) * score_scale).astype(jnp.bfloat16)
        dk_here = jnp.einsum("hgqmk,qhgd->mkhd", grad_low, q_here, precision=highest) * score_scale
        dv_here = jnp.einsum("hgqmk,qhgd->mkhd", weights_low, g_here, precision=highest)
        dkv_acc = dkv_acc.at[listed].add(jnp.stack([dk_here, dv_here], axis=3))
        return dkv_acc, (out_here, dq_here)

    start = jnp.zeros((NB, BLK, KVH, 2, HD), jnp.float32)
    dkv_pack, (out_pack, dq_pack) = lax.scan(one_block, start, positions)
    attn_out = out_pack[block_order].reshape(TOKENS, QH * HD)
    grad_query = dq_pack[block_order].reshape(TOKENS, QH * HD)
    grad_keyval = dkv_pack[block_order].reshape(TOKENS, KVH * 2 * HD)
    return attn_out, grad_query, grad_keyval
```

```python
import functools
import math

import jax
import jax.numpy as jnp
from jax import lax
from jax.experimental import pallas as pl
from jax.experimental.pallas import tpu as pltpu
from jax.sharding import PartitionSpec as P

QH = 64
KVH = 8
HD = 128
BLK = 128
PAIR = 2 * BLK

very_negative = -1e30
score_scale = HD ** (-0.5)
exponent_scale = score_scale * math.log2(math.e)


def attend(
    kv_heads, group_size,
    list_ref, count_ref, order_ref, seg_ref, q_ref, kv_ref, g_ref,
    out_ref, dq_ref, dkv_ref,
    place, kv_turned, score_buf, weight_buf, ds_buf, q_rows, g_rows, g_cols,
    out_acc, dq_acc, top_buf, sum_buf, bias_buf, dkv_acc,
):
    block_total = order_ref.shape[0]
    row_total = group_size * BLK
    chunks = [slice(at, at + PAIR) for at in range(0, row_total, PAIR)]
    heads = [slice(at, at + BLK) for at in range(0, row_total, BLK)]
    me = lax.axis_index("ctx")
    f32 = jnp.float32
    nn = (((1,), (0,)), ((), ()))
    nt = (((1,), (1,)), ((), ()))

    def dot(a, b, dims=nn):
        return lax.dot_general(a, b, dims, preferred_element_type=f32)

    def block_rows(j):
        return pl.ds(pl.multiple_of(j * BLK, BLK), BLK)

    def prepare(j, carry):
        place[order_ref[j]] = j
        for part in range(2 * kv_heads):
            columns = slice(part * HD, (part + 1) * HD)
            kv_turned[part, j] = kv_ref[block_rows(j), columns].T
        dkv_acc[block_rows(j), :] = jnp.zeros((BLK, dkv_acc.shape[1]), f32)
        return carry

    lax.fori_loop(0, block_total, prepare, 0)

    def one(step, carry):
        half = lax.rem(step, 2)
        n = lax.div(step, 2)
        rows = block_rows(half)
        own = order_ref[2 * me + half]
        count = count_ref[own]
        odd = lax.rem(count, 2)
        pairs = lax.div(count + 1, 2)
        key_cols = pl.ds(pl.multiple_of(n * 2 * HD, HD), HD)
        value_cols = pl.ds(pl.multiple_of(n * 2 * HD + HD, HD), HD)

        def head_cols(j):
            return pl.ds(pl.multiple_of(n * row_total + j * HD, HD), HD)

        def other(t):
            t = jnp.maximum(t, 0)
            before = list_ref[own, jnp.maximum(t - 1, 0)]
            return place[jnp.where(before < own, before, list_ref[own, t])]

        def places(r, first):
            here = place[own] if first else other(2 * r - odd)
            return here, other(2 * r + 1 - odd)

        def pair_of(a, b, columns):
            return jnp.concatenate(
                [kv_ref[block_rows(a), columns], kv_ref[block_rows(b), columns]], axis=0
            )

        def each_pair(body):
            body(0, True)

            def later(r, carry):
                body(r, False)
                return carry

            lax.fori_loop(1, pairs, later, 0)

        for j, cut in enumerate(heads):
            q_rows[cut, :] = q_ref[rows, head_cols(j)]
            g_cols[:, cut] = g_ref[rows, head_cols(j)].T
        seg_row = jnp.broadcast_to(seg_ref[pl.ds(own, 1), :].astype(f32), (BLK, BLK))
        key_pos = lax.broadcasted_iota(jnp.int32, (BLK, BLK), 0)
        query_pos = lax.broadcasted_iota(jnp.int32, (BLK, BLK), 1)
        intra = (key_pos <= query_pos) & (seg_row == seg_row.T)
        bias_buf[:BLK, :] = jnp.where(intra, 0.0, very_negative)
        bias_buf[BLK:, :] = jnp.zeros((BLK, BLK), f32) + jnp.where(odd == 1, very_negative, 0.0)
        top_buf[...] = jnp.full(top_buf.shape, very_negative, f32)
        sum_buf[...] = jnp.zeros(sum_buf.shape, f32)
        out_acc[...] = jnp.zeros(out_acc.shape, f32)
        dq_acc[...] = jnp.zeros(dq_acc.shape, f32)

        def score_pass(r, first):
            a, b = places(r, first)
            keys = pair_of(a, b, key_cols)
            for cut in chunks:
                scores = dot(keys, q_rows[cut, :], nt)
                if first:
                    scores = scores + jnp.concatenate([bias_buf[...]] * (PAIR // BLK), axis=1)
                score_buf[r, :, cut] = scores
                folded = jnp.max(scores.reshape(PAIR // 8, 8, PAIR), axis=0)
                top_buf[:, cut] = jnp.maximum(top_buf[:, cut], folded)

        each_pair(score_pass)
        top = jnp.max(top_buf[...], axis=0, keepdims=True) * exponent_scale

        def value_pass(r, first):
            a, b = places(r, first)
            values = jnp.concatenate(
                [kv_turned[2 * n + 1, a], kv_turned[2 * n + 1, b]], axis=1
            )
            for cut in chunks:
                weights = jnp.exp2(score_buf[r, :, cut] * exponent_scale - top[:, cut])
                sum_buf[:, cut] += jnp.sum(weights.reshape(PAIR // 8, 8, PAIR), axis=0)
                low = weights.astype(jnp.bfloat16)
                weight_buf[r, :, cut] = low
                out_acc[:, cut] += dot(values, low)

        each_pair(value_pass)
        inverse = 1.0 / jnp.sum(sum_buf[...], axis=0, keepdims=True)
        deltas = []
        for j, cut in enumerate(heads):
            out_head = out_acc[:, cut] * inverse[:, cut]
            out_ref[rows, head_cols(j)] = out_head.T.astype(jnp.bfloat16)
            g_head = g_cols[:, cut].astype(f32)
            rounded = out_head.astype(jnp.bfloat16).astype(f32)
            deltas.append(jnp.sum(g_head * rounded, axis=0, keepdims=True) * inverse[:, cut])
            g_low = (g_head * inverse[:, cut]).astype(jnp.bfloat16)
            g_cols[:, cut] = g_low
            g_rows[cut, :] = g_low.T
        delta = jnp.concatenate(deltas, axis=1)

        def grad_pass(r, first):
            a, b = places(r, first)
            values = pair_of(a, b, value_cols)
            keys = jnp.concatenate([kv_turned[2 * n, a], kv_turned[2 * n, b]], axis=1)
            for cut in chunks:
                grad_weights = dot(values, g_cols[:, cut])
                shifted = (grad_weights - delta[:, cut]).astype(jnp.bfloat16)
                grad_scores = weight_buf[r, :, cut] * shifted
                ds_buf[:, cut] = grad_scores
                dq_acc[:, cut] += dot(keys, grad_scores)
            dk = dot(ds_buf[...], q_rows[...])
            dv = dot(weight_buf[r], g_rows[...])
            dkv_acc[block_rows(a), key_cols] += dk[:BLK]
            dkv_acc[block_rows(b), key_cols] += dk[BLK:]
            dkv_acc[block_rows(a), value_cols] += dv[:BLK]
            dkv_acc[block_rows(b), value_cols] += dv[BLK:]

        each_pair(grad_pass)
        for j, cut in enumerate(heads):
            dq_ref[rows, head_cols(j)] = (dq_acc[:, cut] * score_scale).T.astype(jnp.bfloat16)
        return carry

    lax.fori_loop(0, 2 * kv_heads, one, 0)

    def finish(j, carry):
        for n in range(kv_heads):
            key_cols = slice(n * 2 * HD, n * 2 * HD + HD)
            value_cols = slice(n * 2 * HD + HD, (n + 1) * 2 * HD)
            dkv_ref[block_rows(j), key_cols] = (
                dkv_acc[block_rows(j), key_cols] * score_scale
            ).astype(jnp.bfloat16)
            dkv_ref[block_rows(j), value_cols] = dkv_acc[block_rows(j), value_cols].astype(
                jnp.bfloat16
            )
        return carry

    lax.fori_loop(0, block_total, finish, 0)


def attention(lists, counts, order, segments, query, kv, grad_out):
    token_total, kv_width = kv.shape
    block_total = token_total // BLK
    kv_heads = kv_width // (2 * HD)
    head_count = query.shape[1] // HD
    group_size = head_count // kv_heads
    row_total = group_size * BLK
    pair_max = (lists.shape[1] + 1) // 2
    bf16, f32 = jnp.bfloat16, jnp.float32
    smem = pl.BlockSpec(memory_space=pltpu.SMEM)
    vmem = pl.BlockSpec(memory_space=pltpu.VMEM)
    return pl.pallas_call(
        functools.partial(attend, kv_heads, group_size),
        out_shape=(
            jax.ShapeDtypeStruct(query.shape, bf16),
            jax.ShapeDtypeStruct(query.shape, bf16),
            jax.ShapeDtypeStruct(kv.shape, bf16),
        ),
        in_specs=[smem] * 3 + [vmem] * 4,
        out_specs=(vmem,) * 3,
        scratch_shapes=[
            pltpu.SMEM((block_total,), jnp.int32),
            pltpu.VMEM((2 * kv_heads, block_total, HD, BLK), bf16),
            pltpu.VMEM((pair_max, PAIR, row_total), f32),
            pltpu.VMEM((pair_max, PAIR, row_total), bf16),
            pltpu.VMEM((PAIR, row_total), bf16),
            pltpu.VMEM((row_total, HD), bf16),
            pltpu.VMEM((row_total, HD), bf16),
            pltpu.VMEM((HD, row_total), bf16),
            pltpu.VMEM((HD, row_total), f32),
            pltpu.VMEM((HD, row_total), f32),
            pltpu.VMEM((8, row_total), f32),
            pltpu.VMEM((8, row_total), f32),
            pltpu.VMEM((PAIR, BLK), f32),
            pltpu.VMEM((token_total, kv_width), f32),
        ],
        compiler_params=pltpu.CompilerParams(vmem_limit_bytes=56 * 2**20),
        cost_estimate=pl.CostEstimate(
            flops=9 * 10**9, bytes_accessed=10 * 2**20, transcendentals=5 * 10**6
        ),
        name="attend",
    )(lists, counts, order, segments, query, kv, grad_out)


def shards(query, keyval, grad_out, vis_blocks, vis_count, segment_ids, block_order):
    head_count = query.shape[1] // HD
    full_group = QH // KVH
    kv_local = max(1, head_count // full_group)
    kv_width = kv_local * 2 * HD
    first_kv = lax.axis_index("head") * head_count // full_group
    mine = lax.dynamic_slice_in_dim(keyval, first_kv * 2 * HD, kv_width, 1)
    gathered = lax.all_gather(mine, "ctx", axis=0, tiled=True)
    attn_out, grad_query, partial_kv = attention(
        vis_blocks, vis_count, block_order, segment_ids.reshape(-1, BLK), query, gathered, grad_out
    )
    summed = lax.psum_scatter(partial_kv, "ctx", scatter_dimension=0, tiled=True)
    if head_count >= full_group:
        result = lax.all_gather(summed, "head", axis=1, tiled=True).astype(jnp.float32)
    else:
        widened = jnp.zeros((summed.shape[0], KVH * 2 * HD), jnp.float32)
        widened = lax.dynamic_update_slice_in_dim(
            widened, summed.astype(jnp.float32), first_kv * 2 * HD, 1
        )
        result = lax.psum(widened.astype(jnp.bfloat16), "head").astype(jnp.float32)
    return (attn_out, grad_query, result)


def solution(mesh):
    placed = (P("ctx", "head"), P("ctx", None), P("ctx", "head"), P(), P(), P(), P())
    return jax.shard_map(
        shards,
        mesh=mesh,
        in_specs=placed,
        out_specs=(P("ctx", "head"), P("ctx", "head"), P("ctx", None)),
        check_vma=False,
    )
```

```python
import functools
import math

import jax
import jax.numpy as jnp
from jax import lax
from jax.experimental import pallas as pl
from jax.experimental.pallas import tpu as pltpu
from jax.sharding import PartitionSpec as P

QH = 64
KVH = 8
HD = 128
BLK = 128
PAIR = 2 * BLK

very_negative = -1e30
score_scale = HD ** (-0.5)
exponent_scale = score_scale * math.log2(math.e)


def attend(
    kv_heads, group_size,
    list_ref, count_ref, order_ref, seg_ref, q_ref, kv_ref, g_ref,
    out_ref, dq_ref, dkv_ref,
    place, kv_turned, score_buf, weight_buf, ds_buf, q_rows, g_rows, g_cols,
    out_acc, dq_acc, top_buf, sum_buf, bias_buf, dkv_acc,
):
    block_total = order_ref.shape[0]
    row_total = group_size * BLK
    chunks = [slice(at, at + PAIR) for at in range(0, row_total, PAIR)]
    heads = [slice(at, at + BLK) for at in range(0, row_total, BLK)]
    me = lax.axis_index("ctx")
    f32 = jnp.float32
    nn = (((1,), (0,)), ((), ()))
    nt = (((1,), (1,)), ((), ()))

    def dot(a, b, dims=nn):
        return lax.dot_general(a, b, dims, preferred_element_type=f32)

    def block_rows(j):
        return pl.ds(pl.multiple_of(j * BLK, BLK), BLK)

    def prepare(j, carry):
        place[order_ref[j]] = j
        for part in range(2 * kv_heads):
            columns = slice(part * HD, (part + 1) * HD)
            kv_turned[part, j] = kv_ref[block_rows(j), columns].T
        dkv_acc[block_rows(j), :] = jnp.zeros((BLK, dkv_acc.shape[1]), f32)
        return carry

    lax.fori_loop(0, block_total, prepare, 0)

    def one(step, carry):
        half = lax.rem(step, 2)
        n = lax.div(step, 2)
        rows = block_rows(half)
        own = order_ref[2 * me + half]
        count = count_ref[own]
        odd = lax.rem(count, 2)
        pairs = lax.div(count + 1, 2)
        key_cols = pl.ds(pl.multiple_of(n * 2 * HD, HD), HD)
        value_cols = pl.ds(pl.multiple_of(n * 2 * HD + HD, HD), HD)

        def head_cols(j):
            return pl.ds(pl.multiple_of(n * row_total + j * HD, HD), HD)

        def other(t):
            t = jnp.maximum(t, 0)
            before = list_ref[own, jnp.maximum(t - 1, 0)]
            return place[jnp.where(before < own, before, list_ref[own, t])]

        def places(r, first):
            here = place[own] if first else other(2 * r - odd)
            return here, other(2 * r + 1 - odd)

        def pair_of(a, b, columns):
            return jnp.concatenate(
                [kv_ref[block_rows(a), columns], kv_ref[block_rows(b), columns]], axis=0
            )

        def each_pair(body):
            body(0, True)

            def later(r, carry):
                body(r, False)
                return carry

            lax.fori_loop(1, pairs, later, 0)

        for j, cut in enumerate(heads):
            q_rows[cut, :] = q_ref[rows, head_cols(j)]
            g_cols[:, cut] = g_ref[rows, head_cols(j)].T
        seg_row = jnp.broadcast_to(seg_ref[pl.ds(own, 1), :].astype(f32), (BLK, BLK))
        key_pos = lax.broadcasted_iota(jnp.int32, (BLK, BLK), 0)
        query_pos = lax.broadcasted_iota(jnp.int32, (BLK, BLK), 1)
        intra = (key_pos <= query_pos) & (seg_row == seg_row.T)
        bias_buf[:BLK, :] = jnp.where(intra, 0.0, very_negative)
        bias_buf[BLK:, :] = jnp.zeros((BLK, BLK), f32) + jnp.where(odd == 1, very_negative, 0.0)
        top_buf[...] = jnp.full(top_buf.shape, very_negative, f32)
        sum_buf[...] = jnp.zeros(sum_buf.shape, f32)
        out_acc[...] = jnp.zeros(out_acc.shape, f32)
        dq_acc[...] = jnp.zeros(dq_acc.shape, f32)

        def score_pass(r, first):
            a, b = places(r, first)
            keys = pair_of(a, b, key_cols)
            for cut in chunks:
                scores = dot(keys, q_rows[cut, :], nt)
                if first:
                    scores = scores + jnp.concatenate([bias_buf[...]] * (PAIR // BLK), axis=1)
                score_buf[r, :, cut] = scores
                folded = jnp.max(scores.reshape(PAIR // 8, 8, PAIR), axis=0)
                top_buf[:, cut] = jnp.maximum(top_buf[:, cut], folded)

        each_pair(score_pass)
        top = jnp.max(top_buf[...], axis=0, keepdims=True) * exponent_scale

        def value_pass(r, first):
            a, b = places(r, first)
            values = jnp.concatenate(
                [kv_turned[2 * n + 1, a], kv_turned[2 * n + 1, b]], axis=1
            )
            for cut in chunks:
                weights = jnp.exp2(score_buf[r, :, cut] * exponent_scale - top[:, cut])
                sum_buf[:, cut] += jnp.sum(weights.reshape(PAIR // 8, 8, PAIR), axis=0)
                low = weights.astype(jnp.bfloat16)
                weight_buf[r, :, cut] = low
                out_acc[:, cut] += dot(values, low)

        each_pair(value_pass)
        inverse = 1.0 / jnp.sum(sum_buf[...], axis=0, keepdims=True)
        deltas = []
        for j, cut in enumerate(heads):
            out_head = out_acc[:, cut] * inverse[:, cut]
            out_ref[rows, head_cols(j)] = out_head.T.astype(jnp.bfloat16)
            g_head = g_cols[:, cut].astype(f32)
            rounded = out_head.astype(jnp.bfloat16).astype(f32)
            deltas.append(jnp.sum(g_head * rounded, axis=0, keepdims=True) * inverse[:, cut])
            g_low = (g_head * inverse[:, cut]).astype(jnp.bfloat16)
            g_cols[:, cut] = g_low
            g_rows[cut, :] = g_low.T
        delta = jnp.concatenate(deltas, axis=1)

        def grad_pass(r, first):
            a, b = places(r, first)
            values = pair_of(a, b, value_cols)
            keys = jnp.concatenate([kv_turned[2 * n, a], kv_turned[2 * n, b]], axis=1)
            for cut in chunks:
                grad_weights = dot(values, g_cols[:, cut])
                shifted = (grad_weights - delta[:, cut]).astype(jnp.bfloat16)
                grad_scores = weight_buf[r, :, cut] * shifted
                ds_buf[:, cut] = grad_scores
                dq_acc[:, cut] += dot(keys, grad_scores)
            dk = dot(ds_buf[...], q_rows[...])
            dv = dot(weight_buf[r], g_rows[...])
            dkv_acc[block_rows(a), key_cols] += dk[:BLK]
            dkv_acc[block_rows(b), key_cols] += dk[BLK:]
            dkv_acc[block_rows(a), value_cols] += dv[:BLK]
            dkv_acc[block_rows(b), value_cols] += dv[BLK:]

        each_pair(grad_pass)
        for j, cut in enumerate(heads):
            dq_ref[rows, head_cols(j)] = (dq_acc[:, cut] * score_scale).T.astype(jnp.bfloat16)
        return carry

    lax.fori_loop(0, 2 * kv_heads, one, 0)

    def finish(j, carry):
        for n in range(kv_heads):
            key_cols = slice(n * 2 * HD, n * 2 * HD + HD)
            value_cols = slice(n * 2 * HD + HD, (n + 1) * 2 * HD)
            dkv_ref[block_rows(j), key_cols] = (
                dkv_acc[block_rows(j), key_cols] * score_scale
            ).astype(jnp.bfloat16)
            dkv_ref[block_rows(j), value_cols] = dkv_acc[block_rows(j), value_cols].astype(
                jnp.bfloat16
            )
        return carry

    lax.fori_loop(0, block_total, finish, 0)


def attention(lists, counts, order, segments, query, kv, grad_out):
    token_total, kv_width = kv.shape
    block_total = token_total // BLK
    kv_heads = kv_width // (2 * HD)
    head_count = query.shape[1] // HD
    group_size = head_count // kv_heads
    row_total = group_size * BLK
    pair_max = (lists.shape[1] + 1) // 2
    bf16, f32 = jnp.bfloat16, jnp.float32
    smem = pl.BlockSpec(memory_space=pltpu.SMEM)
    vmem = pl.BlockSpec(memory_space=pltpu.VMEM)
    return pl.pallas_call(
        functools.partial(attend, kv_heads, group_size),
        out_shape=(
            jax.ShapeDtypeStruct(query.shape, bf16),
            jax.ShapeDtypeStruct(query.shape, bf16),
            jax.ShapeDtypeStruct(kv.shape, bf16),
        ),
        in_specs=[smem] * 3 + [vmem] * 4,
        out_specs=(vmem,) * 3,
        scratch_shapes=[
            pltpu.SMEM((block_total,), jnp.int32),
            pltpu.VMEM((2 * kv_heads, block_total, HD, BLK), bf16),
            pltpu.VMEM((pair_max, PAIR, row_total), f32),
            pltpu.VMEM((pair_max, PAIR, row_total), bf16),
            pltpu.VMEM((PAIR, row_total), bf16),
            pltpu.VMEM((row_total, HD), bf16),
            pltpu.VMEM((row_total, HD), bf16),
            pltpu.VMEM((HD, row_total), bf16),
            pltpu.VMEM((HD, row_total), f32),
            pltpu.VMEM((HD, row_total), f32),
            pltpu.VMEM((8, row_total), f32),
            pltpu.VMEM((8, row_total), f32),
            pltpu.VMEM((PAIR, BLK), f32),
            pltpu.VMEM((token_total, kv_width), f32),
        ],
        compiler_params=pltpu.CompilerParams(vmem_limit_bytes=56 * 2**20),
        cost_estimate=pl.CostEstimate(
            flops=9 * 10**9, bytes_accessed=10 * 2**20, transcendentals=5 * 10**6
        ),
        name="attend",
    )(lists, counts, order, segments, query, kv, grad_out)


MESH = pl.DeviceIdType.MESH
PIECES = 2


def greet(conditions):
    barrier = pltpu.get_barrier_semaphore()
    for present, target in conditions:
        @pl.when(present)
        def _():
            pl.semaphore_signal(barrier, inc=1, device_id=target, device_id_type=MESH)
    pl.semaphore_wait(barrier, sum(present.astype(jnp.int32) for present, _ in conditions))


def line_place(line):
    c = lax.axis_index("ctx")
    z, x = lax.div(c, 2), lax.rem(c, 2)
    return c, z, x, z < line - 1, z > 0


def collect(line, head_count, kv_ref, out_ref, send_sems, recv_sems, local_sem):
    c, z, x, has_up, has_down = line_place(line)
    targets = ({"ctx": c + 2}, {"ctx": c - 2}, {"ctx": c + 1 - 2 * x})
    present = (has_up, has_down, z >= 0)
    shard, width = kv_ref.shape[0], out_ref.shape[1]
    size = shard // PIECES
    first = lax.div(lax.axis_index("head") * head_count, QH // KVH) * 2 * HD
    columns = pl.ds(pl.multiple_of(first, HD), width)
    greet(list(zip(present, targets)))

    def landing(slot, piece):
        return out_ref.at[pl.ds(pl.multiple_of(slot * shard + piece * size, size), size)]

    def copy(slot, piece, way, own=False):
        here = landing(slot, piece)
        source = kv_ref.at[pl.ds(piece * size, size), columns] if own else here
        return pltpu.make_async_remote_copy(
            src_ref=source,
            dst_ref=here,
            send_sem=send_sems.at[slot, piece, way],
            recv_sem=recv_sems.at[slot, piece],
            device_id=targets[way],
            device_id_type=MESH,
        )

    for piece in range(PIECES):
        for way in range(3):
            @pl.when(present[way])
            def _():
                copy(c, piece, way, True).start()
    local = pltpu.make_async_copy(
        kv_ref.at[:, columns],
        out_ref.at[pl.ds(pl.multiple_of(c * shard, shard), shard)],
        local_sem,
    )
    local.start()

    for d in range(1, line):
        for piece in range(PIECES):
            @pl.when(z - d >= 0)
            def _():
                copy(c - 2 * d, piece, 2).wait_recv()

                @pl.when(has_up)
                def _():
                    copy(c - 2 * d, piece, 0).start()

                copy(c - 2 * d, piece, 2).start()

            @pl.when(z + d <= line - 1)
            def _():
                copy(c + 2 * d, piece, 2).wait_recv()

                @pl.when(has_down)
                def _():
                    copy(c + 2 * d, piece, 1).start()

                copy(c + 2 * d, piece, 2).start()

    for other in range(line):
        for piece in range(PIECES):
            copy(2 * other + 1 - x, piece, 2).wait_recv()
            copy(2 * other + x, piece, 2).wait_send()
    for piece in range(PIECES):
        for way in range(2):
            @pl.when(present[way])
            def _():
                copy(c, piece, way, True).wait_send()
    for d in range(1, line):
        for piece in range(PIECES):
            @pl.when((z - d >= 0) & has_up)
            def _():
                copy(c - 2 * d, piece, 0).wait_send()

            @pl.when((z + d <= line - 1) & has_down)
            def _():
                copy(c + 2 * d, piece, 1).wait_send()
    local.wait()


def gather_tokens(keyval, line, head_count, width):
    shard = keyval.shape[0]
    anywhere = pl.BlockSpec(memory_space=pl.ANY)
    return pl.pallas_call(
        functools.partial(collect, line, head_count),
        out_shape=jax.ShapeDtypeStruct((2 * line * shard, width), keyval.dtype),
        in_specs=[anywhere],
        out_specs=anywhere,
        scratch_shapes=[
            pltpu.SemaphoreType.DMA((2 * line, PIECES, 3)),
            pltpu.SemaphoreType.DMA((2 * line, PIECES)),
            pltpu.SemaphoreType.DMA,
        ],
        compiler_params=pltpu.CompilerParams(collective_id=0, has_side_effects=True),
        name="collect",
    )(keyval)


def spread(
    line, exchange, part_ref, out_ref,
    across_buf, up_in, down_in, up_out, down_out,
    across_send, across_recv, up_send, up_recv, down_send, down_recv, head_send, head_recv,
):
    c, z, x, has_up, has_down = line_place(line)
    shard, width = part_ref.shape[0] // (2 * line), part_ref.shape[1]
    size = shard // PIECES
    f32, bf16 = jnp.float32, jnp.bfloat16
    beside = {"ctx": c + 1 - 2 * x}
    always = z >= 0
    people = [(has_up, {"ctx": c + 2}), (has_down, {"ctx": c - 2}), (always, beside)]
    h = lax.axis_index("head")
    core = lax.rem(h, 2)
    twin, facing = h + 1 - 2 * core, lax.rem(h + 2, 4)
    if exchange:
        people += [(always, {"head": twin}), (always, {"head": facing})]
    greet(people)

    def part_rows(place, piece):
        return pl.ds(pl.multiple_of(place * shard + piece * size, size), size)

    def across(zs, piece):
        return pltpu.make_async_remote_copy(
            src_ref=part_ref.at[part_rows(2 * zs + 1 - x, piece)],
            dst_ref=across_buf.at[zs, piece],
            send_sem=across_send.at[zs, piece],
            recv_sem=across_recv.at[zs, piece],
            device_id=beside,
            device_id_type=MESH,
        )

    def up(zs, piece):
        return pltpu.make_async_remote_copy(
            src_ref=up_out.at[zs, piece],
            dst_ref=up_in.at[zs, piece],
            send_sem=up_send.at[zs, piece],
            recv_sem=up_recv.at[zs, piece],
            device_id={"ctx": c + 2},
            device_id_type=MESH,
        )

    def down(zs, piece):
        return pltpu.make_async_remote_copy(
            src_ref=down_out.at[zs, piece],
            dst_ref=down_in.at[zs, piece],
            send_sem=down_send.at[zs, piece],
            recv_sem=down_recv.at[zs, piece],
            device_id={"ctx": c - 2},
            device_id_type=MESH,
        )

    def to_head(slot, piece, way):
        here = out_ref.at[
            pl.ds(piece * size, size), pl.ds(pl.multiple_of(slot * width, width), width)
        ]
        return pltpu.make_async_remote_copy(
            src_ref=here,
            dst_ref=here,
            send_sem=head_send.at[piece, way],
            recv_sem=head_recv.at[piece, slot],
            device_id={"head": facing if way == 0 else twin},
            device_id_type=MESH,
        )

    def by_distance(body):
        for d in range(line - 1, 0, -1):
            @pl.when(z + d <= line - 1)
            def _():
                body(z + d, 1)

            @pl.when(z - d >= 0)
            def _():
                body(z - d, -1)

    for piece in range(PIECES):
        by_distance(lambda zs, side: across(zs, piece).start())
        across(z, piece).start()

    def add_along(zs, side, piece):
        across(zs, piece).wait_recv()
        total = part_ref[part_rows(2 * zs + x, piece), :].astype(f32)
        total = total + across_buf[zs, piece].astype(f32)
        buf, inward, move = (up_out, up_in, up) if side > 0 else (down_out, down_in, down)
        more = has_down if side > 0 else has_up

        @pl.when(more)
        def _():
            move(zs, piece).wait_recv()
            buf[zs, piece] = (total + inward[zs, piece].astype(f32)).astype(bf16)

        @pl.when(jnp.logical_not(more))
        def _():
            buf[zs, piece] = total.astype(bf16)

        move(zs, piece).start()

    def finish(piece):
        across(z, piece).wait_recv()
        total = part_ref[part_rows(c, piece), :].astype(f32) + across_buf[z, piece].astype(f32)
        rows = pl.ds(piece * size, size)
        if exchange:
            columns = pl.ds(pl.multiple_of(h * width, width), width)
        else:
            columns = slice(None)

        @pl.when(has_down & has_up)
        def _():
            up(z, piece).wait_recv()
            down(z, piece).wait_recv()
            arrived = up_in[z, piece].astype(f32) + down_in[z, piece].astype(f32)
            out_ref[rows, columns] = (total + arrived).astype(bf16)

        @pl.when(has_down & jnp.logical_not(has_up))
        def _():
            up(z, piece).wait_recv()
            out_ref[rows, columns] = (total + up_in[z, piece].astype(f32)).astype(bf16)

        @pl.when(has_up & jnp.logical_not(has_down))
        def _():
            down(z, piece).wait_recv()
            out_ref[rows, columns] = (total + down_in[z, piece].astype(f32)).astype(bf16)

        if exchange:
            to_head(h, piece, 0).start()
            to_head(h, piece, 1).start()

    for piece in range(PIECES):
        by_distance(lambda zs, side: add_along(zs, side, piece))
        finish(piece)
    if exchange:
        for piece in range(PIECES):
            to_head(facing, piece, 2).wait_recv()
            to_head(facing, piece, 2).start()
        for piece in range(PIECES):
            to_head(twin, piece, 1).wait_recv()
            to_head(lax.rem(twin + 2, 4), piece, 2).wait_recv()
            to_head(h, piece, 0).wait_send()
            to_head(h, piece, 1).wait_send()
            to_head(facing, piece, 2).wait_send()
    for piece in range(PIECES):
        by_distance(lambda zs, side: (up if side > 0 else down)(zs, piece).wait_send())
        for zs in range(line):
            across(zs, piece).wait_send()


def reduce_tokens(partial_kv, line, exchange):
    shard, width = partial_kv.shape[0] // (2 * line), partial_kv.shape[1]
    columns = width * (4 if exchange else 1)
    vmem = pl.BlockSpec(memory_space=pltpu.VMEM)
    slots = pltpu.VMEM((line, PIECES, shard // PIECES, width), partial_kv.dtype)
    sems = pltpu.SemaphoreType.DMA((line, PIECES))
    return pl.pallas_call(
        functools.partial(spread, line, exchange),
        out_shape=jax.ShapeDtypeStruct((shard, columns), partial_kv.dtype),
        in_specs=[vmem],
        out_specs=vmem,
        scratch_shapes=[slots] * 5 + [sems] * 6 + [
            pltpu.SemaphoreType.DMA((PIECES, 3)),
            pltpu.SemaphoreType.DMA((PIECES, 4)),
        ],
        compiler_params=pltpu.CompilerParams(
            collective_id=1, has_side_effects=True, vmem_limit_bytes=40 * 2**20
        ),
        name="spread",
    )(partial_kv)


def shards(query, keyval, grad_out, vis_blocks, vis_count, segment_ids, block_order):
    head_count = query.shape[1] // HD
    full_group = QH // KVH
    kv_local = max(1, head_count // full_group)
    kv_width = kv_local * 2 * HD
    line = lax.axis_size("ctx") // 2
    exchange = lax.axis_size("head") == 4 and head_count >= full_group
    gathered = gather_tokens(keyval, line, head_count, kv_width)
    attn_out, grad_query, partial_kv = attention(
        vis_blocks, vis_count, block_order, segment_ids.reshape(-1, BLK), query, gathered, grad_out
    )
    summed = reduce_tokens(partial_kv, line, exchange)
    if exchange:
        result = summed.astype(jnp.float32)
    elif head_count >= full_group:
        result = lax.all_gather(summed, "head", axis=1, tiled=True).astype(jnp.float32)
    else:
        first_kv = lax.axis_index("head") * head_count // full_group
        widened = jnp.zeros((summed.shape[0], KVH * 2 * HD), jnp.float32)
        widened = lax.dynamic_update_slice_in_dim(
            widened, summed.astype(jnp.float32), first_kv * 2 * HD, 1
        )
        result = lax.psum(widened.astype(jnp.bfloat16), "head").astype(jnp.float32)
    return (attn_out, grad_query, result)


def solution(mesh):
    placed = (P("ctx", "head"), P("ctx", None), P("ctx", "head"), P(), P(), P(), P())
    return jax.shard_map(
        shards,
        mesh=mesh,
        in_specs=placed,
        out_specs=(P("ctx", "head"), P("ctx", "head"), P("ctx", None)),
        check_vma=False,
    )
```

```python
import functools
import math

import jax
import jax.numpy as jnp
from jax import lax
from jax.experimental import pallas as pl
from jax.experimental.pallas import tpu as pltpu
from jax.sharding import PartitionSpec as P

QH = 64
KVH = 8
HD = 128
BLK = 128
PAIR = 2 * BLK

very_negative = -1e30
score_scale = HD ** (-0.5)
exponent_scale = score_scale * math.log2(math.e)


def attend(
    group_size, kv_count, chained, dkv_count,
    list_ref, count_ref, order_ref, seg_ref, q_ref, g_ref, *rest,
):
    kv_refs, rest = rest[:kv_count], rest[kv_count + (2 if chained else 0):]
    out_ref, dq_ref, dkv_refs, rest = rest[0], rest[1], rest[2:2 + dkv_count], rest[2 + dkv_count:]
    (
        place, kv_whole, kv_turned, score_buf, weight_buf, ds_buf, q_rows, g_rows, g_cols,
        out_acc, dq_acc, top_buf, sum_buf, bias_buf, dkv_acc,
    ) = rest
    key_cols, value_cols = slice(0, HD), slice(HD, 2 * HD)
    block_total = order_ref.shape[0]
    row_total = group_size * BLK
    chunks = [slice(at, at + PAIR) for at in range(0, row_total, PAIR)]
    heads = [slice(at, at + BLK) for at in range(0, row_total, BLK)]
    me = lax.axis_index("ctx")
    f32 = jnp.float32
    nn = (((1,), (0,)), ((), ()))
    nt = (((1,), (1,)), ((), ()))

    def dot(a, b, dims=nn):
        return lax.dot_general(a, b, dims, preferred_element_type=f32)

    def block_rows(j):
        return pl.ds(pl.multiple_of(j * BLK, BLK), BLK)

    kv_ref = kv_refs[0] if kv_count == 1 else kv_whole
    if kv_count > 1:
        for k, ref in enumerate(kv_refs):
            source = lax.rem(me - k + kv_count, kv_count)
            size = ref.shape[0]
            kv_whole[pl.ds(pl.multiple_of(source * size, size), size), :] = ref[...]

    def prepare(j, carry):
        place[order_ref[j]] = j
        for part in range(2):
            columns = slice(part * HD, (part + 1) * HD)
            kv_turned[part, j] = kv_ref[block_rows(j), columns].T
        dkv_acc[block_rows(j), :] = jnp.zeros((BLK, dkv_acc.shape[1]), f32)
        return carry

    lax.fori_loop(0, block_total, prepare, 0)

    def one(half, carry):
        rows = block_rows(half)
        own = order_ref[2 * me + half]
        count = count_ref[own]
        odd = lax.rem(count, 2)
        pairs = lax.div(count + 1, 2)

        def head_cols(j):
            return slice(j * HD, (j + 1) * HD)

        def other(t):
            t = jnp.maximum(t, 0)
            before = list_ref[own, jnp.maximum(t - 1, 0)]
            return place[jnp.where(before < own, before, list_ref[own, t])]

        def places(r, first):
            here = place[own] if first else other(2 * r - odd)
            return here, other(2 * r + 1 - odd)

        def pair_of(a, b, columns):
            return jnp.concatenate(
                [kv_ref[block_rows(a), columns], kv_ref[block_rows(b), columns]], axis=0
            )

        def each_pair(body):
            body(0, True)

            def later(r, carry):
                body(r, False)
                return carry

            lax.fori_loop(1, pairs, later, 0)

        for j, cut in enumerate(heads):
            q_rows[cut, :] = q_ref[rows, head_cols(j)]
            g_cols[:, cut] = g_ref[rows, head_cols(j)].T
        seg_row = jnp.broadcast_to(seg_ref[pl.ds(own, 1), :].astype(f32), (BLK, BLK))
        key_pos = lax.broadcasted_iota(jnp.int32, (BLK, BLK), 0)
        query_pos = lax.broadcasted_iota(jnp.int32, (BLK, BLK), 1)
        intra = (key_pos <= query_pos) & (seg_row == seg_row.T)
        bias_buf[:BLK, :] = jnp.where(intra, 0.0, very_negative)
        bias_buf[BLK:, :] = jnp.zeros((BLK, BLK), f32) + jnp.where(odd == 1, very_negative, 0.0)
        top_buf[...] = jnp.full(top_buf.shape, very_negative, f32)
        sum_buf[...] = jnp.zeros(sum_buf.shape, f32)
        out_acc[...] = jnp.zeros(out_acc.shape, f32)
        dq_acc[...] = jnp.zeros(dq_acc.shape, f32)

        def score_pass(r, first):
            a, b = places(r, first)
            keys = pair_of(a, b, key_cols)
            for cut in chunks:
                scores = dot(keys, q_rows[cut, :], nt)
                if first:
                    scores = scores + jnp.concatenate([bias_buf[...]] * (PAIR // BLK), axis=1)
                score_buf[r, :, cut] = scores
                folded = jnp.max(scores.reshape(PAIR // 8, 8, PAIR), axis=0)
                top_buf[:, cut] = jnp.maximum(top_buf[:, cut], folded)

        each_pair(score_pass)
        top = jnp.max(top_buf[...], axis=0, keepdims=True) * exponent_scale

        def value_pass(r, first):
            a, b = places(r, first)
            values = jnp.concatenate(
                [kv_turned[1, a], kv_turned[1, b]], axis=1
            )
            for cut in chunks:
                weights = jnp.exp2(score_buf[r, :, cut] * exponent_scale - top[:, cut])
                sum_buf[:, cut] += jnp.sum(weights.reshape(PAIR // 8, 8, PAIR), axis=0)
                low = weights.astype(jnp.bfloat16)
                weight_buf[r, :, cut] = low
                out_acc[:, cut] += dot(values, low)

        each_pair(value_pass)
        inverse = 1.0 / jnp.sum(sum_buf[...], axis=0, keepdims=True)
        deltas = []
        for j, cut in enumerate(heads):
            out_head = out_acc[:, cut] * inverse[:, cut]
            out_ref[rows, head_cols(j)] = out_head.T.astype(jnp.bfloat16)
            g_head = g_cols[:, cut].astype(f32)
            rounded = out_head.astype(jnp.bfloat16).astype(f32)
            deltas.append(jnp.sum(g_head * rounded, axis=0, keepdims=True) * inverse[:, cut])
            g_low = (g_head * inverse[:, cut]).astype(jnp.bfloat16)
            g_cols[:, cut] = g_low
            g_rows[cut, :] = g_low.T
        delta = jnp.concatenate(deltas, axis=1)

        def grad_pass(r, first):
            a, b = places(r, first)
            values = pair_of(a, b, value_cols)
            keys = jnp.concatenate([kv_turned[0, a], kv_turned[0, b]], axis=1)
            for cut in chunks:
                grad_weights = dot(values, g_cols[:, cut])
                shifted = (grad_weights - delta[:, cut]).astype(jnp.bfloat16)
                grad_scores = weight_buf[r, :, cut] * shifted
                ds_buf[:, cut] = grad_scores
                dq_acc[:, cut] += dot(keys, grad_scores)
            dk = dot(ds_buf[...], q_rows[...])
            dv = dot(weight_buf[r], g_rows[...])
            dkv_acc[block_rows(a), key_cols] += dk[:BLK]
            dkv_acc[block_rows(b), key_cols] += dk[BLK:]
            dkv_acc[block_rows(a), value_cols] += dv[:BLK]
            dkv_acc[block_rows(b), value_cols] += dv[BLK:]

        each_pair(grad_pass)
        for j, cut in enumerate(heads):
            dq_ref[rows, head_cols(j)] = (dq_acc[:, cut] * score_scale).T.astype(jnp.bfloat16)
        return carry

    lax.fori_loop(0, 2, one, 0)
    for k, ref in enumerate(dkv_refs):
        size = ref.shape[0]
        target = lax.rem(me + k, dkv_count) if dkv_count > 1 else 0
        for at in range(0, size, BLK):
            rows = pl.ds(pl.multiple_of(target * size + at, BLK), BLK)
            ref[at:at + BLK, key_cols] = (dkv_acc[rows, key_cols] * score_scale).astype(
                jnp.bfloat16
            )
            ref[at:at + BLK, value_cols] = dkv_acc[rows, value_cols].astype(jnp.bfloat16)


def attention(lists, counts, order, segments, query, grad_out, kv_list, turn, turns, earlier, cut):
    token_total = order.shape[0] * BLK
    kv_width = 2 * HD
    block_total = token_total // BLK
    columns = query.shape[1] // turns
    group_size = columns // HD
    row_total = group_size * BLK
    pair_max = (lists.shape[1] + 1) // 2
    bf16, f32 = jnp.bfloat16, jnp.float32
    smem = pl.BlockSpec(memory_space=pltpu.SMEM)
    vmem = pl.BlockSpec(memory_space=pltpu.VMEM)
    block = pl.BlockSpec((query.shape[0], columns), lambda step: (0, turn))
    wide = jax.ShapeDtypeStruct(query.shape, bf16)
    earlier = list(earlier)
    before = 6 + len(kv_list)
    return pl.pallas_call(
        functools.partial(attend, group_size, len(kv_list), bool(earlier), cut),
        grid=(1,),
        out_shape=[wide, wide]
        + [jax.ShapeDtypeStruct((token_total // cut, kv_width), bf16)] * cut,
        in_specs=[smem] * 3 + [vmem] + [block] * 2 + [vmem] * len(kv_list)
        + [pl.BlockSpec(memory_space=pl.ANY)] * len(earlier),
        out_specs=[block] * 2 + [vmem] * cut,
        input_output_aliases={before: 0, before + 1: 1} if earlier else {},
        scratch_shapes=[
            pltpu.SMEM((block_total,), jnp.int32),
            pltpu.VMEM((token_total if len(kv_list) > 1 else BLK, kv_width), bf16),
            pltpu.VMEM((2, block_total, HD, BLK), bf16),
            pltpu.VMEM((pair_max, PAIR, row_total), f32),
            pltpu.VMEM((pair_max, PAIR, row_total), bf16),
            pltpu.VMEM((PAIR, row_total), bf16),
            pltpu.VMEM((row_total, HD), bf16),
            pltpu.VMEM((row_total, HD), bf16),
            pltpu.VMEM((HD, row_total), bf16),
            pltpu.VMEM((HD, row_total), f32),
            pltpu.VMEM((HD, row_total), f32),
            pltpu.VMEM((8, row_total), f32),
            pltpu.VMEM((8, row_total), f32),
            pltpu.VMEM((PAIR, BLK), f32),
            pltpu.VMEM((token_total, kv_width), f32),
        ],
        compiler_params=pltpu.CompilerParams(vmem_limit_bytes=56 * 2**20),
        cost_estimate=pl.CostEstimate(
            flops=20 * 10**9, bytes_accessed=10 * 2**20, transcendentals=5 * 10**6
        ),
        name="attend",
    )(lists, counts, order, segments, query, grad_out, *kv_list, *earlier)


MESH = pl.DeviceIdType.MESH
PIECES = 2


def greet(conditions):
    barrier = pltpu.get_barrier_semaphore()
    for present, target in conditions:
        @pl.when(present)
        def _():
            pl.semaphore_signal(barrier, inc=1, device_id=target, device_id_type=MESH)
    pl.semaphore_wait(barrier, sum(present.astype(jnp.int32) for present, _ in conditions))


def line_place(line):
    c = lax.axis_index("ctx")
    z, x = lax.div(c, 2), lax.rem(c, 2)
    return c, z, x, z < line - 1, z > 0


def collect(line, head_count, kv_ref, out_ref, send_sems, recv_sems, local_sem):
    c, z, x, has_up, has_down = line_place(line)
    targets = ({"ctx": c + 2}, {"ctx": c - 2}, {"ctx": c + 1 - 2 * x})
    present = (has_up, has_down, z >= 0)
    shard, width = kv_ref.shape[0], out_ref.shape[1]
    size = shard // PIECES
    first = lax.div(lax.axis_index("head") * head_count, QH // KVH) * 2 * HD
    columns = pl.ds(pl.multiple_of(first, HD), width)
    greet(list(zip(present, targets)))

    def landing(slot, piece):
        return out_ref.at[pl.ds(pl.multiple_of(slot * shard + piece * size, size), size)]

    def copy(slot, piece, way, own=False):
        here = landing(slot, piece)
        source = kv_ref.at[pl.ds(piece * size, size), columns] if own else here
        return pltpu.make_async_remote_copy(
            src_ref=source,
            dst_ref=here,
            send_sem=send_sems.at[slot, piece, way],
            recv_sem=recv_sems.at[slot, piece],
            device_id=targets[way],
            device_id_type=MESH,
        )

    for piece in range(PIECES):
        for way in range(3):
            @pl.when(present[way])
            def _():
                copy(c, piece, way, True).start()
    local = pltpu.make_async_copy(
        kv_ref.at[:, columns],
        out_ref.at[pl.ds(pl.multiple_of(c * shard, shard), shard)],
        local_sem,
    )
    local.start()

    for d in range(1, line):
        for piece in range(PIECES):
            @pl.when(z - d >= 0)
            def _():
                copy(c - 2 * d, piece, 2).wait_recv()

                @pl.when(has_up)
                def _():
                    copy(c - 2 * d, piece, 0).start()

                copy(c - 2 * d, piece, 2).start()

            @pl.when(z + d <= line - 1)
            def _():
                copy(c + 2 * d, piece, 2).wait_recv()

                @pl.when(has_down)
                def _():
                    copy(c + 2 * d, piece, 1).start()

                copy(c + 2 * d, piece, 2).start()

    for other in range(line):
        for piece in range(PIECES):
            copy(2 * other + 1 - x, piece, 2).wait_recv()
            copy(2 * other + x, piece, 2).wait_send()
    for piece in range(PIECES):
        for way in range(2):
            @pl.when(present[way])
            def _():
                copy(c, piece, way, True).wait_send()
    for d in range(1, line):
        for piece in range(PIECES):
            @pl.when((z - d >= 0) & has_up)
            def _():
                copy(c - 2 * d, piece, 0).wait_send()

            @pl.when((z + d <= line - 1) & has_down)
            def _():
                copy(c + 2 * d, piece, 1).wait_send()
    local.wait()


def gather_tokens(keyval, line, head_count, width):
    shard = keyval.shape[0]
    anywhere = pl.BlockSpec(memory_space=pl.ANY)
    return pl.pallas_call(
        functools.partial(collect, line, head_count),
        out_shape=jax.ShapeDtypeStruct((2 * line * shard, width), keyval.dtype),
        in_specs=[anywhere],
        out_specs=anywhere,
        scratch_shapes=[
            pltpu.SemaphoreType.DMA((2 * line, PIECES, 3)),
            pltpu.SemaphoreType.DMA((2 * line, PIECES)),
            pltpu.SemaphoreType.DMA,
        ],
        compiler_params=pltpu.CompilerParams(collective_id=0, has_side_effects=True),
        name="collect",
    )(keyval)


def spread(
    line, exchange, early_count, part_ref, *rest,
):
    early_refs, out_ref = rest[:early_count], rest[early_count]
    (
    across_buf, up_in, down_in, up_out, down_out,
    across_send, across_recv, up_send, up_recv, down_send, down_recv, head_send, head_recv,
    ) = rest[early_count + 1:]
    c, z, x, has_up, has_down = line_place(line)
    shard, width = part_ref.shape[0] // (2 * line), part_ref.shape[1]
    size = shard // PIECES
    f32, bf16 = jnp.float32, jnp.bfloat16
    beside = {"ctx": c + 1 - 2 * x}
    always = z >= 0
    people = [(has_up, {"ctx": c + 2}), (has_down, {"ctx": c - 2}), (always, beside)]
    h = lax.axis_index("head")
    core = lax.rem(h, 2)
    twin, facing = h + 1 - 2 * core, lax.rem(h + 2, 4)
    if exchange:
        people += [(always, {"head": twin}), (always, {"head": facing})]
    greet(people)

    def part_rows(place, piece):
        return pl.ds(pl.multiple_of(place * shard + piece * size, size), size)

    def across(zs, piece):
        return pltpu.make_async_remote_copy(
            src_ref=part_ref.at[part_rows(2 * zs + 1 - x, piece)],
            dst_ref=across_buf.at[zs, piece],
            send_sem=across_send.at[zs, piece],
            recv_sem=across_recv.at[zs, piece],
            device_id=beside,
            device_id_type=MESH,
        )

    def up(zs, piece):
        return pltpu.make_async_remote_copy(
            src_ref=up_out.at[zs, piece],
            dst_ref=up_in.at[zs, piece],
            send_sem=up_send.at[zs, piece],
            recv_sem=up_recv.at[zs, piece],
            device_id={"ctx": c + 2},
            device_id_type=MESH,
        )

    def down(zs, piece):
        return pltpu.make_async_remote_copy(
            src_ref=down_out.at[zs, piece],
            dst_ref=down_in.at[zs, piece],
            send_sem=down_send.at[zs, piece],
            recv_sem=down_recv.at[zs, piece],
            device_id={"ctx": c - 2},
            device_id_type=MESH,
        )

    per_head = width * (2 if early_count else 1)
    offset = per_head - width

    def to_head(slot, piece, way):
        early = piece == PIECES
        here = out_ref.at[
            pl.ds(0, shard) if early else pl.ds(piece * size, size),
            pl.ds(pl.multiple_of(slot * per_head + (0 if early else offset), width), width),
        ]
        return pltpu.make_async_remote_copy(
            src_ref=here,
            dst_ref=here,
            send_sem=head_send.at[piece, way],
            recv_sem=head_recv.at[piece, slot],
            device_id={"head": facing if way == 0 else twin},
            device_id_type=MESH,
        )

    def by_distance(body):
        for d in range(line - 1, 0, -1):
            @pl.when(z + d <= line - 1)
            def _():
                body(z + d, 1)

            @pl.when(z - d >= 0)
            def _():
                body(z - d, -1)

    for piece in range(PIECES):
        by_distance(lambda zs, side: across(zs, piece).start())
        across(z, piece).start()

    if early_count:
        done = early_refs[0][...].astype(f32)
        for ref in early_refs[1:]:
            done = done + ref[...].astype(f32)
        out_ref[:, pl.ds(pl.multiple_of(h * per_head, width), width)] = done.astype(bf16)
        to_head(h, PIECES, 0).start()
        to_head(h, PIECES, 1).start()

    def add_along(zs, side, piece):
        across(zs, piece).wait_recv()
        total = part_ref[part_rows(2 * zs + x, piece), :].astype(f32)
        total = total + across_buf[zs, piece].astype(f32)
        buf, inward, move = (up_out, up_in, up) if side > 0 else (down_out, down_in, down)
        more = has_down if side > 0 else has_up

        @pl.when(more)
        def _():
            move(zs, piece).wait_recv()
            buf[zs, piece] = (total + inward[zs, piece].astype(f32)).astype(bf16)

        @pl.when(jnp.logical_not(more))
        def _():
            buf[zs, piece] = total.astype(bf16)

        move(zs, piece).start()

    def finish(piece):
        across(z, piece).wait_recv()
        total = part_ref[part_rows(c, piece), :].astype(f32) + across_buf[z, piece].astype(f32)
        rows = pl.ds(piece * size, size)
        if exchange:
            columns = pl.ds(pl.multiple_of(h * per_head + offset, width), width)
        else:
            columns = slice(None)

        @pl.when(has_down & has_up)
        def _():
            up(z, piece).wait_recv()
            down(z, piece).wait_recv()
            arrived = up_in[z, piece].astype(f32) + down_in[z, piece].astype(f32)
            out_ref[rows, columns] = (total + arrived).astype(bf16)

        @pl.when(has_down & jnp.logical_not(has_up))
        def _():
            up(z, piece).wait_recv()
            out_ref[rows, columns] = (total + up_in[z, piece].astype(f32)).astype(bf16)

        @pl.when(has_up & jnp.logical_not(has_down))
        def _():
            down(z, piece).wait_recv()
            out_ref[rows, columns] = (total + down_in[z, piece].astype(f32)).astype(bf16)

        if exchange:
            to_head(h, piece, 0).start()
            to_head(h, piece, 1).start()

    for piece in range(PIECES):
        by_distance(lambda zs, side: add_along(zs, side, piece))
        finish(piece)
    if exchange:
        head_pieces = ([PIECES] if early_count else []) + list(range(PIECES))
        for piece in head_pieces:
            to_head(facing, piece, 2).wait_recv()
            to_head(facing, piece, 2).start()
        for piece in head_pieces:
            to_head(twin, piece, 1).wait_recv()
            to_head(lax.rem(twin + 2, 4), piece, 2).wait_recv()
            to_head(h, piece, 0).wait_send()
            to_head(h, piece, 1).wait_send()
            to_head(facing, piece, 2).wait_send()
    for piece in range(PIECES):
        by_distance(lambda zs, side: (up if side > 0 else down)(zs, piece).wait_send())
        for zs in range(line):
            across(zs, piece).wait_send()


def reduce_tokens(partial_kv, early, line, exchange):
    shard, width = partial_kv.shape[0] // (2 * line), partial_kv.shape[1]
    columns = width * (4 if exchange else 1) * (2 if early else 1)
    vmem = pl.BlockSpec(memory_space=pltpu.VMEM)
    slots = pltpu.VMEM((line, PIECES, shard // PIECES, width), partial_kv.dtype)
    sems = pltpu.SemaphoreType.DMA((line, PIECES))
    return pl.pallas_call(
        functools.partial(spread, line, exchange, len(early)),
        out_shape=jax.ShapeDtypeStruct((shard, columns), partial_kv.dtype),
        in_specs=[vmem] * (1 + len(early)),
        out_specs=vmem,
        scratch_shapes=[slots] * 5 + [sems] * 6 + [
            pltpu.SemaphoreType.DMA((PIECES + 1, 3)),
            pltpu.SemaphoreType.DMA((PIECES + 1, 4)),
        ],
        compiler_params=pltpu.CompilerParams(
            collective_id=1, has_side_effects=True, vmem_limit_bytes=40 * 2**20
        ),
        name="spread",
    )(partial_kv, *early)


def shards(query, keyval, grad_out, vis_blocks, vis_count, segment_ids, block_order):
    head_count = query.shape[1] // HD
    full_group = QH // KVH
    kv_local = max(1, head_count // full_group)
    kv_width = kv_local * 2 * HD
    line = lax.axis_size("ctx") // 2
    exchange = lax.axis_size("head") == 4 and head_count >= full_group
    devices = 2 * line
    width = 2 * HD
    gathered = gather_tokens(keyval, line, head_count, width)
    given = (vis_blocks, vis_count, block_order, segment_ids.reshape(-1, BLK), query, grad_out)

    def shifted(array, k):
        return lax.ppermute(array, "ctx", [(i, (i + k) % devices) for i in range(devices)])

    if exchange and kv_local == 2:
        held, gathered = lax.optimization_barrier((keyval, gathered))
        second = lax.dynamic_slice_in_dim(held, lax.axis_index("head") * kv_width + width, width, 1)
        seconds = [second] + [shifted(second, k) for k in range(1, devices)]
        attn_out, grad_query, *parts = attention(*given, [gathered], 0, 2, (), devices)
        early = [parts[0]] + [shifted(parts[k], k) for k in range(1, devices)]
        attn_out, grad_query, partial_kv = attention(
            *given, seconds, 1, 2, (attn_out, grad_query), 1
        )
    else:
        assert kv_local == 1
        early = []
        attn_out, grad_query, partial_kv = attention(*given, [gathered], 0, 1, (), 1)
    summed = reduce_tokens(partial_kv, early, line, exchange)
    if exchange:
        result = summed.astype(jnp.float32)
    elif head_count >= full_group:
        result = lax.all_gather(summed, "head", axis=1, tiled=True).astype(jnp.float32)
    else:
        first_kv = lax.axis_index("head") * head_count // full_group
        widened = jnp.zeros((summed.shape[0], KVH * 2 * HD), jnp.float32)
        widened = lax.dynamic_update_slice_in_dim(
            widened, summed.astype(jnp.float32), first_kv * 2 * HD, 1
        )
        result = lax.psum(widened.astype(jnp.bfloat16), "head").astype(jnp.float32)
    return (attn_out, grad_query, result)


def solution(mesh):
    placed = (P("ctx", "head"), P("ctx", None), P("ctx", "head"), P(), P(), P(), P())
    return jax.shard_map(
        shards,
        mesh=mesh,
        in_specs=placed,
        out_specs=(P("ctx", "head"), P("ctx", "head"), P("ctx", None)),
        check_vma=False,
    )
```

```python
import functools
import math

import jax
import jax.numpy as jnp
from jax import lax
from jax.experimental import pallas as pl
from jax.experimental.pallas import tpu as pltpu
from jax.sharding import PartitionSpec as P

QH = 64
KVH = 8
HD = 128
BLK = 128
PAIR = 2 * BLK

very_negative = -1e30
score_scale = HD ** (-0.5)
exponent_scale = score_scale * math.log2(math.e)


def attend(
    kv_heads, group_size,
    list_ref, count_ref, order_ref, seg_ref, q_ref, kv_ref, g_ref,
    out_ref, dq_ref, dkv_ref,
    place, kv_turned, score_buf, weight_buf, ds_buf, q_rows, g_rows, g_cols,
    out_acc, dq_acc, top_buf, sum_buf, bias_buf, dkv_acc,
):
    block_total = order_ref.shape[0]
    group_rows = group_size * BLK
    row_total = kv_heads * group_rows
    chunks = [slice(at, at + PAIR) for at in range(0, row_total, PAIR)]
    heads = [slice(at, at + BLK) for at in range(0, row_total, BLK)]
    me = lax.axis_index("ctx")
    f32 = jnp.float32
    nn = (((1,), (0,)), ((), ()))
    nt = (((1,), (1,)), ((), ()))

    def dot(a, b, dims=nn):
        return lax.dot_general(a, b, dims, preferred_element_type=f32)

    def block_rows(j):
        return pl.ds(pl.multiple_of(j * BLK, BLK), BLK)

    def prepare(j, carry):
        place[order_ref[j]] = j
        for part in range(2 * kv_heads):
            columns = slice(part * HD, (part + 1) * HD)
            kv_turned[part, j] = kv_ref[block_rows(j), columns].T
        dkv_acc[block_rows(j), :] = jnp.zeros((BLK, dkv_acc.shape[1]), f32)
        return carry

    lax.fori_loop(0, block_total, prepare, 0)

    def one(half, carry):
        rows = block_rows(half)
        own = order_ref[2 * me + half]
        count = count_ref[own]
        odd = lax.rem(count, 2)
        pairs = lax.div(count + 1, 2)
        key_cols = [slice(n * 2 * HD, n * 2 * HD + HD) for n in range(kv_heads)]
        value_cols = [slice(n * 2 * HD + HD, (n + 1) * 2 * HD) for n in range(kv_heads)]

        def head_cols(j):
            return slice(j * HD, (j + 1) * HD)

        def other(t):
            t = jnp.maximum(t, 0)
            before = list_ref[own, jnp.maximum(t - 1, 0)]
            return place[jnp.where(before < own, before, list_ref[own, t])]

        def places(r, first):
            here = place[own] if first else other(2 * r - odd)
            return here, other(2 * r + 1 - odd)

        def pair_of(a, b, columns):
            return jnp.concatenate(
                [kv_ref[block_rows(a), columns], kv_ref[block_rows(b), columns]], axis=0
            )

        def turned_pair(part, a, b):
            return jnp.concatenate([kv_turned[part, a], kv_turned[part, b]], axis=1)

        def each_pair(body):
            body(0, True)

            def later(r, carry):
                body(r, False)
                return carry

            lax.fori_loop(1, pairs, later, 0)

        for j, cut in enumerate(heads):
            q_rows[cut, :] = q_ref[rows, head_cols(j)]
            g_cols[:, cut] = g_ref[rows, head_cols(j)].T
        seg_row = jnp.broadcast_to(seg_ref[pl.ds(own, 1), :].astype(f32), (BLK, BLK))
        key_pos = lax.broadcasted_iota(jnp.int32, (BLK, BLK), 0)
        query_pos = lax.broadcasted_iota(jnp.int32, (BLK, BLK), 1)
        intra = (key_pos <= query_pos) & (seg_row == seg_row.T)
        bias_buf[:BLK, :] = jnp.where(intra, 0.0, very_negative)
        bias_buf[BLK:, :] = jnp.zeros((BLK, BLK), f32) + jnp.where(odd == 1, very_negative, 0.0)
        top_buf[...] = jnp.full(top_buf.shape, very_negative, f32)
        sum_buf[...] = jnp.zeros(sum_buf.shape, f32)
        out_acc[...] = jnp.zeros(out_acc.shape, f32)
        dq_acc[...] = jnp.zeros(dq_acc.shape, f32)

        def score_pass(r, first):
            a, b = places(r, first)
            keys = [pair_of(a, b, columns) for columns in key_cols]
            for cut in chunks:
                scores = dot(keys[cut.start // group_rows], q_rows[cut, :], nt)
                if first:
                    scores = scores + jnp.concatenate([bias_buf[...]] * (PAIR // BLK), axis=1)
                score_buf[r, :, cut] = scores
                folded = jnp.max(scores.reshape(PAIR // 8, 8, PAIR), axis=0)
                top_buf[:, cut] = jnp.maximum(top_buf[:, cut], folded)

        each_pair(score_pass)
        top = jnp.max(top_buf[...], axis=0, keepdims=True) * exponent_scale

        def value_pass(r, first):
            a, b = places(r, first)
            values = [turned_pair(2 * n + 1, a, b) for n in range(kv_heads)]
            for cut in chunks:
                weights = jnp.exp2(score_buf[r, :, cut] * exponent_scale - top[:, cut])
                sum_buf[:, cut] += jnp.sum(weights.reshape(PAIR // 8, 8, PAIR), axis=0)
                low = weights.astype(jnp.bfloat16)
                weight_buf[r, :, cut] = low
                out_acc[:, cut] += dot(values[cut.start // group_rows], low)

        each_pair(value_pass)
        inverse = 1.0 / jnp.sum(sum_buf[...], axis=0, keepdims=True)
        deltas = []
        for j, cut in enumerate(heads):
            out_head = out_acc[:, cut] * inverse[:, cut]
            out_ref[rows, head_cols(j)] = out_head.T.astype(jnp.bfloat16)
            g_head = g_cols[:, cut].astype(f32)
            rounded = out_head.astype(jnp.bfloat16).astype(f32)
            deltas.append(jnp.sum(g_head * rounded, axis=0, keepdims=True) * inverse[:, cut])
            g_low = (g_head * inverse[:, cut]).astype(jnp.bfloat16)
            g_cols[:, cut] = g_low
            g_rows[cut, :] = g_low.T
        delta = jnp.concatenate(deltas, axis=1)

        def grad_pass(r, first):
            a, b = places(r, first)
            values = [pair_of(a, b, columns) for columns in value_cols]
            keys = [turned_pair(2 * n, a, b) for n in range(kv_heads)]
            for cut in chunks:
                grad_weights = dot(values[cut.start // group_rows], g_cols[:, cut])
                shifted = (grad_weights - delta[:, cut]).astype(jnp.bfloat16)
                grad_scores = weight_buf[r, :, cut] * shifted
                ds_buf[:, cut] = grad_scores
                dq_acc[:, cut] += dot(keys[cut.start // group_rows], grad_scores)
            for n in range(kv_heads):
                group = slice(n * group_rows, (n + 1) * group_rows)
                dk = dot(ds_buf[:, group], q_rows[group, :])
                dv = dot(weight_buf[r, :, group], g_rows[group, :])
                dkv_acc[block_rows(a), key_cols[n]] += dk[:BLK]
                dkv_acc[block_rows(b), key_cols[n]] += dk[BLK:]
                dkv_acc[block_rows(a), value_cols[n]] += dv[:BLK]
                dkv_acc[block_rows(b), value_cols[n]] += dv[BLK:]

        each_pair(grad_pass)
        for j, cut in enumerate(heads):
            dq_ref[rows, head_cols(j)] = (dq_acc[:, cut] * score_scale).T.astype(jnp.bfloat16)
        return carry

    lax.fori_loop(0, 2, one, 0)

    def finish(j, carry):
        for n in range(kv_heads):
            key_cols = slice(n * 2 * HD, n * 2 * HD + HD)
            value_cols = slice(n * 2 * HD + HD, (n + 1) * 2 * HD)
            dkv_ref[block_rows(j), key_cols] = (
                dkv_acc[block_rows(j), key_cols] * score_scale
            ).astype(jnp.bfloat16)
            dkv_ref[block_rows(j), value_cols] = dkv_acc[block_rows(j), value_cols].astype(
                jnp.bfloat16
            )
        return carry

    lax.fori_loop(0, block_total, finish, 0)


def attention(lists, counts, order, segments, query, kv, grad_out):
    token_total, kv_width = kv.shape
    block_total = token_total // BLK
    kv_heads = kv_width // (2 * HD)
    head_count = query.shape[1] // HD
    group_size = head_count // kv_heads
    row_total = head_count * BLK
    pair_max = (lists.shape[1] + 1) // 2
    bf16, f32 = jnp.bfloat16, jnp.float32
    smem = pl.BlockSpec(memory_space=pltpu.SMEM)
    vmem = pl.BlockSpec(memory_space=pltpu.VMEM)
    return pl.pallas_call(
        functools.partial(attend, kv_heads, group_size),
        out_shape=(
            jax.ShapeDtypeStruct(query.shape, bf16),
            jax.ShapeDtypeStruct(query.shape, bf16),
            jax.ShapeDtypeStruct(kv.shape, bf16),
        ),
        in_specs=[smem] * 3 + [vmem] * 4,
        out_specs=(vmem,) * 3,
        scratch_shapes=[
            pltpu.SMEM((block_total,), jnp.int32),
            pltpu.VMEM((2 * kv_heads, block_total, HD, BLK), bf16),
            pltpu.VMEM((pair_max, PAIR, row_total), f32),
            pltpu.VMEM((pair_max, PAIR, row_total), bf16),
            pltpu.VMEM((PAIR, row_total), bf16),
            pltpu.VMEM((row_total, HD), bf16),
            pltpu.VMEM((row_total, HD), bf16),
            pltpu.VMEM((HD, row_total), bf16),
            pltpu.VMEM((HD, row_total), f32),
            pltpu.VMEM((HD, row_total), f32),
            pltpu.VMEM((8, row_total), f32),
            pltpu.VMEM((8, row_total), f32),
            pltpu.VMEM((PAIR, BLK), f32),
            pltpu.VMEM((token_total, kv_width), f32),
        ],
        compiler_params=pltpu.CompilerParams(vmem_limit_bytes=56 * 2**20),
        cost_estimate=pl.CostEstimate(
            flops=9 * 10**9, bytes_accessed=10 * 2**20, transcendentals=5 * 10**6
        ),
        name="attend",
    )(lists, counts, order, segments, query, kv, grad_out)


MESH = pl.DeviceIdType.MESH
PIECES = 2


def greet(conditions):
    barrier = pltpu.get_barrier_semaphore()
    for present, target in conditions:
        @pl.when(present)
        def _():
            pl.semaphore_signal(barrier, inc=1, device_id=target, device_id_type=MESH)
    pl.semaphore_wait(barrier, sum(present.astype(jnp.int32) for present, _ in conditions))


def line_place(line):
    c = lax.axis_index("ctx")
    z, x = lax.div(c, 2), lax.rem(c, 2)
    return c, z, x, z < line - 1, z > 0


def collect(line, head_count, kv_ref, out_ref, send_sems, recv_sems, local_sem):
    c, z, x, has_up, has_down = line_place(line)
    targets = ({"ctx": c + 2}, {"ctx": c - 2}, {"ctx": c + 1 - 2 * x})
    present = (has_up, has_down, z >= 0)
    shard, width = kv_ref.shape[0], out_ref.shape[1]
    size = shard // PIECES
    first = lax.div(lax.axis_index("head") * head_count, QH // KVH) * 2 * HD
    columns = pl.ds(pl.multiple_of(first, HD), width)
    greet(list(zip(present, targets)))

    def landing(slot, piece):
        return out_ref.at[pl.ds(pl.multiple_of(slot * shard + piece * size, size), size)]

    def copy(slot, piece, way, own=False):
        here = landing(slot, piece)
        source = kv_ref.at[pl.ds(piece * size, size), columns] if own else here
        return pltpu.make_async_remote_copy(
            src_ref=source,
            dst_ref=here,
            send_sem=send_sems.at[slot, piece, way],
            recv_sem=recv_sems.at[slot, piece],
            device_id=targets[way],
            device_id_type=MESH,
        )

    for piece in range(PIECES):
        for way in range(3):
            @pl.when(present[way])
            def _():
                copy(c, piece, way, True).start()
    local = pltpu.make_async_copy(
        kv_ref.at[:, columns],
        out_ref.at[pl.ds(pl.multiple_of(c * shard, shard), shard)],
        local_sem,
    )
    local.start()

    for d in range(1, line):
        for piece in range(PIECES):
            @pl.when(z - d >= 0)
            def _():
                copy(c - 2 * d, piece, 2).wait_recv()

                @pl.when(has_up)
                def _():
                    copy(c - 2 * d, piece, 0).start()

                copy(c - 2 * d, piece, 2).start()

            @pl.when(z + d <= line - 1)
            def _():
                copy(c + 2 * d, piece, 2).wait_recv()

                @pl.when(has_down)
                def _():
                    copy(c + 2 * d, piece, 1).start()

                copy(c + 2 * d, piece, 2).start()

    for other in range(line):
        for piece in range(PIECES):
            copy(2 * other + 1 - x, piece, 2).wait_recv()
            copy(2 * other + x, piece, 2).wait_send()
    for piece in range(PIECES):
        for way in range(2):
            @pl.when(present[way])
            def _():
                copy(c, piece, way, True).wait_send()
    for d in range(1, line):
        for piece in range(PIECES):
            @pl.when((z - d >= 0) & has_up)
            def _():
                copy(c - 2 * d, piece, 0).wait_send()

            @pl.when((z + d <= line - 1) & has_down)
            def _():
                copy(c + 2 * d, piece, 1).wait_send()
    local.wait()


def gather_tokens(keyval, line, head_count, width):
    shard = keyval.shape[0]
    anywhere = pl.BlockSpec(memory_space=pl.ANY)
    return pl.pallas_call(
        functools.partial(collect, line, head_count),
        out_shape=jax.ShapeDtypeStruct((2 * line * shard, width), keyval.dtype),
        in_specs=[anywhere],
        out_specs=anywhere,
        scratch_shapes=[
            pltpu.SemaphoreType.DMA((2 * line, PIECES, 3)),
            pltpu.SemaphoreType.DMA((2 * line, PIECES)),
            pltpu.SemaphoreType.DMA,
        ],
        compiler_params=pltpu.CompilerParams(collective_id=0, has_side_effects=True),
        name="collect",
    )(keyval)


def spread(
    line, exchange, part_ref, out_ref,
    across_buf, up_in, down_in, up_out, down_out,
    across_send, across_recv, up_send, up_recv, down_send, down_recv, head_send, head_recv,
):
    c, z, x, has_up, has_down = line_place(line)
    shard, width = part_ref.shape[0] // (2 * line), part_ref.shape[1]
    size = shard // PIECES
    f32, bf16 = jnp.float32, jnp.bfloat16
    beside = {"ctx": c + 1 - 2 * x}
    always = z >= 0
    people = [(has_up, {"ctx": c + 2}), (has_down, {"ctx": c - 2}), (always, beside)]
    h = lax.axis_index("head")
    core = lax.rem(h, 2)
    twin, facing = h + 1 - 2 * core, lax.rem(h + 2, 4)
    if exchange:
        people += [(always, {"head": twin}), (always, {"head": facing})]
    greet(people)

    def part_rows(place, piece):
        return pl.ds(pl.multiple_of(place * shard + piece * size, size), size)

    def across(zs, piece):
        return pltpu.make_async_remote_copy(
            src_ref=part_ref.at[part_rows(2 * zs + 1 - x, piece)],
            dst_ref=across_buf.at[zs, piece],
            send_sem=across_send.at[zs, piece],
            recv_sem=across_recv.at[zs, piece],
            device_id=beside,
            device_id_type=MESH,
        )

    def up(zs, piece):
        return pltpu.make_async_remote_copy(
            src_ref=up_out.at[zs, piece],
            dst_ref=up_in.at[zs, piece],
            send_sem=up_send.at[zs, piece],
            recv_sem=up_recv.at[zs, piece],
            device_id={"ctx": c + 2},
            device_id_type=MESH,
        )

    def down(zs, piece):
        return pltpu.make_async_remote_copy(
            src_ref=down_out.at[zs, piece],
            dst_ref=down_in.at[zs, piece],
            send_sem=down_send.at[zs, piece],
            recv_sem=down_recv.at[zs, piece],
            device_id={"ctx": c - 2},
            device_id_type=MESH,
        )

    def to_head(slot, piece, way):
        here = out_ref.at[
            pl.ds(piece * size, size), pl.ds(pl.multiple_of(slot * width, width), width)
        ]
        return pltpu.make_async_remote_copy(
            src_ref=here,
            dst_ref=here,
            send_sem=head_send.at[piece, way],
            recv_sem=head_recv.at[piece, slot],
            device_id={"head": facing if way == 0 else twin},
            device_id_type=MESH,
        )

    lower, upper = z, line - 1 - z
    lone = jnp.abs(upper - lower)

    def place_at(k):
        step = jnp.maximum(k - lone, 0)
        d = jnp.minimum(lower, upper) - lax.div(step, 2)
        paired = jnp.where(lax.rem(step, 2) == 0, z + d, z - d)
        return jnp.where(k < lone, jnp.where(upper > lower, line - 1 - k, k), paired)

    turns = [(k, piece) for piece in range(PIECES) for k in range(line)]
    ahead = 2

    def launch(turn):
        if turn < len(turns):
            k, piece = turns[turn]
            across(place_at(k), piece).start()

    def add_along(zs, side, piece):
        total = part_ref[part_rows(2 * zs + x, piece), :].astype(f32)
        total = total + across_buf[zs, piece].astype(f32)
        buf, inward, move = (up_out, up_in, up) if side > 0 else (down_out, down_in, down)
        more = has_down if side > 0 else has_up

        @pl.when(more)
        def _():
            move(zs, piece).wait_recv()
            buf[zs, piece] = (total + inward[zs, piece].astype(f32)).astype(bf16)

        @pl.when(jnp.logical_not(more))
        def _():
            buf[zs, piece] = total.astype(bf16)

        move(zs, piece).start()

    def finish(piece):
        total = part_ref[part_rows(c, piece), :].astype(f32) + across_buf[z, piece].astype(f32)
        rows = pl.ds(piece * size, size)
        if exchange:
            columns = pl.ds(pl.multiple_of(h * width, width), width)
        else:
            columns = slice(None)

        @pl.when(has_down & has_up)
        def _():
            up(z, piece).wait_recv()
            down(z, piece).wait_recv()
            arrived = up_in[z, piece].astype(f32) + down_in[z, piece].astype(f32)
            out_ref[rows, columns] = (total + arrived).astype(bf16)

        @pl.when(has_down & jnp.logical_not(has_up))
        def _():
            up(z, piece).wait_recv()
            out_ref[rows, columns] = (total + up_in[z, piece].astype(f32)).astype(bf16)

        @pl.when(has_up & jnp.logical_not(has_down))
        def _():
            down(z, piece).wait_recv()
            out_ref[rows, columns] = (total + down_in[z, piece].astype(f32)).astype(bf16)

        if exchange:
            to_head(h, piece, 0).start()
            to_head(h, piece, 1).start()

    for turn in range(ahead):
        launch(turn)
    for turn, (k, piece) in enumerate(turns):
        zs = place_at(k)
        across(zs, piece).wait_recv()
        across(zs, piece).wait_send()
        launch(turn + ahead)
        if k == line - 1:
            finish(piece)
        else:
            @pl.when(zs > z)
            def _():
                add_along(zs, 1, piece)

            @pl.when(zs < z)
            def _():
                add_along(zs, -1, piece)

    if exchange:
        for piece in range(PIECES):
            to_head(facing, piece, 2).wait_recv()
            to_head(facing, piece, 2).start()
        for piece in range(PIECES):
            to_head(twin, piece, 1).wait_recv()
            to_head(lax.rem(twin + 2, 4), piece, 2).wait_recv()
            to_head(h, piece, 0).wait_send()
            to_head(h, piece, 1).wait_send()
            to_head(facing, piece, 2).wait_send()
    for piece in range(PIECES):
        for zs in range(line):
            @pl.when(zs > z)
            def _():
                up(zs, piece).wait_send()

            @pl.when(zs < z)
            def _():
                down(zs, piece).wait_send()


def reduce_tokens(partial_kv, line, exchange):
    shard, width = partial_kv.shape[0] // (2 * line), partial_kv.shape[1]
    columns = width * (4 if exchange else 1)
    vmem = pl.BlockSpec(memory_space=pltpu.VMEM)
    slots = pltpu.VMEM((line, PIECES, shard // PIECES, width), partial_kv.dtype)
    sems = pltpu.SemaphoreType.DMA((line, PIECES))
    return pl.pallas_call(
        functools.partial(spread, line, exchange),
        out_shape=jax.ShapeDtypeStruct((shard, columns), partial_kv.dtype),
        in_specs=[vmem],
        out_specs=vmem,
        scratch_shapes=[slots] * 5 + [sems] * 6 + [
            pltpu.SemaphoreType.DMA((PIECES, 3)),
            pltpu.SemaphoreType.DMA((PIECES, 4)),
        ],
        compiler_params=pltpu.CompilerParams(
            collective_id=1, has_side_effects=True, vmem_limit_bytes=40 * 2**20
        ),
        name="spread",
    )(partial_kv)


def shards(query, keyval, grad_out, vis_blocks, vis_count, segment_ids, block_order):
    head_count = query.shape[1] // HD
    full_group = QH // KVH
    kv_local = max(1, head_count // full_group)
    kv_width = kv_local * 2 * HD
    line = lax.axis_size("ctx") // 2
    exchange = lax.axis_size("head") == 4 and head_count >= full_group
    gathered = gather_tokens(keyval, line, head_count, kv_width)
    attn_out, grad_query, partial_kv = attention(
        vis_blocks, vis_count, block_order, segment_ids.reshape(-1, BLK), query, gathered, grad_out
    )
    summed = reduce_tokens(partial_kv, line, exchange)
    if exchange:
        result = summed.astype(jnp.float32)
    elif head_count >= full_group:
        result = lax.all_gather(summed, "head", axis=1, tiled=True).astype(jnp.float32)
    else:
        first_kv = lax.axis_index("head") * head_count // full_group
        widened = jnp.zeros((summed.shape[0], KVH * 2 * HD), jnp.float32)
        widened = lax.dynamic_update_slice_in_dim(
            widened, summed.astype(jnp.float32), first_kv * 2 * HD, 1
        )
        result = lax.psum(widened.astype(jnp.bfloat16), "head").astype(jnp.float32)
    return (attn_out, grad_query, result)


def solution(mesh):
    placed = (P("ctx", "head"), P("ctx", None), P("ctx", "head"), P(), P(), P(), P())
    return jax.shard_map(
        shards,
        mesh=mesh,
        in_specs=placed,
        out_specs=(P("ctx", "head"), P("ctx", "head"), P("ctx", None)),
        check_vma=False,
    )
```

```python
import functools
import math

import jax
import jax.numpy as jnp
from jax import lax
from jax.experimental import pallas as pl
from jax.experimental.pallas import tpu as pltpu
from jax.sharding import PartitionSpec as P

QH = 64
KVH = 8
HD = 128
BLK = 128
PAIR = 2 * BLK

very_negative = -1e30
score_scale = HD ** (-0.5)
exponent_scale = score_scale * math.log2(math.e)


def attend(
    kv_heads, group_size,
    list_ref, count_ref, order_ref, seg_ref, q_ref, kv_ref, g_ref,
    out_ref, dq_ref, dkv_ref,
    place, kv_turned, score_buf, weight_buf, ds_buf, q_rows, g_rows, g_cols,
    out_acc, dq_acc, top_buf, sum_buf, bias_buf, dkv_acc,
):
    block_total = order_ref.shape[0]
    group_rows = group_size * BLK
    row_total = kv_heads * group_rows
    chunks = [slice(at, at + PAIR) for at in range(0, row_total, PAIR)]
    heads = [slice(at, at + BLK) for at in range(0, row_total, BLK)]
    me = lax.axis_index("ctx")
    f32 = jnp.float32
    nn = (((1,), (0,)), ((), ()))
    nt = (((1,), (1,)), ((), ()))

    def dot(a, b, dims=nn):
        return lax.dot_general(a, b, dims, preferred_element_type=f32)

    def block_rows(j):
        return pl.ds(pl.multiple_of(j * BLK, BLK), BLK)

    def prepare(j, carry):
        place[order_ref[j]] = j
        for part in range(2 * kv_heads):
            columns = slice(part * HD, (part + 1) * HD)
            kv_turned[part, j] = kv_ref[block_rows(j), columns].T
        dkv_acc[block_rows(j), :] = jnp.zeros((BLK, dkv_acc.shape[1]), f32)
        return carry

    lax.fori_loop(0, block_total, prepare, 0)

    def one(half, carry):
        rows = block_rows(half)
        own = order_ref[2 * me + half]
        count = count_ref[own]
        odd = lax.rem(count, 2)
        pairs = lax.div(count + 1, 2)
        key_cols = [slice(n * 2 * HD, n * 2 * HD + HD) for n in range(kv_heads)]
        value_cols = [slice(n * 2 * HD + HD, (n + 1) * 2 * HD) for n in range(kv_heads)]

        def head_cols(j):
            return slice(j * HD, (j + 1) * HD)

        def other(t):
            t = jnp.maximum(t, 0)
            before = list_ref[own, jnp.maximum(t - 1, 0)]
            return place[jnp.where(before < own, before, list_ref[own, t])]

        def places(r, first):
            here = place[own] if first else other(2 * r - odd)
            return here, other(2 * r + 1 - odd)

        def pair_of(a, b, columns):
            return jnp.concatenate(
                [kv_ref[block_rows(a), columns], kv_ref[block_rows(b), columns]], axis=0
            )

        def turned_pair(part, a, b):
            return jnp.concatenate([kv_turned[part, a], kv_turned[part, b]], axis=1)

        def each_pair(body):
            body(0, True)

            def later(r, carry):
                body(r, False)
                return carry

            lax.fori_loop(1, pairs, later, 0)

        for j, cut in enumerate(heads):
            q_rows[cut, :] = q_ref[rows, head_cols(j)]
            g_cols[:, cut] = g_ref[rows, head_cols(j)].T
        seg_row = jnp.broadcast_to(seg_ref[pl.ds(own, 1), :].astype(f32), (BLK, BLK))
        key_pos = lax.broadcasted_iota(jnp.int32, (BLK, BLK), 0)
        query_pos = lax.broadcasted_iota(jnp.int32, (BLK, BLK), 1)
        intra = (key_pos <= query_pos) & (seg_row == seg_row.T)
        bias_buf[:BLK, :] = jnp.where(intra, 0.0, very_negative)
        bias_buf[BLK:, :] = jnp.zeros((BLK, BLK), f32) + jnp.where(odd == 1, very_negative, 0.0)
        top_buf[...] = jnp.full(top_buf.shape, very_negative, f32)
        sum_buf[...] = jnp.zeros(sum_buf.shape, f32)
        out_acc[...] = jnp.zeros(out_acc.shape, f32)
        dq_acc[...] = jnp.zeros(dq_acc.shape, f32)

        def score_pass(r, first):
            a, b = places(r, first)
            keys = [pair_of(a, b, columns) for columns in key_cols]
            for cut in chunks:
                scores = dot(keys[cut.start // group_rows], q_rows[cut, :], nt)
                if first:
                    scores = scores + jnp.concatenate([bias_buf[...]] * (PAIR // BLK), axis=1)
                score_buf[r, :, cut] = scores
                folded = jnp.max(scores.reshape(PAIR // 8, 8, PAIR), axis=0)
                top_buf[:, cut] = jnp.maximum(top_buf[:, cut], folded)

        each_pair(score_pass)
        top = jnp.max(top_buf[...], axis=0, keepdims=True) * exponent_scale

        def value_pass(r, first):
            a, b = places(r, first)
            values = [turned_pair(2 * n + 1, a, b) for n in range(kv_heads)]
            for cut in chunks:
                weights = jnp.exp2(score_buf[r, :, cut] * exponent_scale - top[:, cut])
                sum_buf[:, cut] += jnp.sum(weights.reshape(PAIR // 8, 8, PAIR), axis=0)
                low = weights.astype(jnp.bfloat16)
                weight_buf[r, :, cut] = low
                out_acc[:, cut] += dot(values[cut.start // group_rows], low)

        each_pair(value_pass)
        inverse = 1.0 / jnp.sum(sum_buf[...], axis=0, keepdims=True)
        deltas = []
        for j, cut in enumerate(heads):
            out_head = out_acc[:, cut] * inverse[:, cut]
            out_ref[rows, head_cols(j)] = out_head.T.astype(jnp.bfloat16)
            g_head = g_cols[:, cut].astype(f32)
            rounded = out_head.astype(jnp.bfloat16).astype(f32)
            deltas.append(jnp.sum(g_head * rounded, axis=0, keepdims=True) * inverse[:, cut])
            g_low = (g_head * inverse[:, cut]).astype(jnp.bfloat16)
            g_cols[:, cut] = g_low
            g_rows[cut, :] = g_low.T
        delta = jnp.concatenate(deltas, axis=1)

        def grad_pass(r, first):
            a, b = places(r, first)
            values = [pair_of(a, b, columns) for columns in value_cols]
            keys = [turned_pair(2 * n, a, b) for n in range(kv_heads)]
            for cut in chunks:
                grad_weights = dot(values[cut.start // group_rows], g_cols[:, cut])
                shifted = (grad_weights - delta[:, cut]).astype(jnp.bfloat16)
                grad_scores = weight_buf[r, :, cut] * shifted
                ds_buf[:, cut] = grad_scores
                dq_acc[:, cut] += dot(keys[cut.start // group_rows], grad_scores)
            for n in range(kv_heads):
                group = slice(n * group_rows, (n + 1) * group_rows)
                dk = dot(ds_buf[:, group], q_rows[group, :])
                dv = dot(weight_buf[r, :, group], g_rows[group, :])
                dkv_acc[block_rows(a), key_cols[n]] += dk[:BLK]
                dkv_acc[block_rows(b), key_cols[n]] += dk[BLK:]
                dkv_acc[block_rows(a), value_cols[n]] += dv[:BLK]
                dkv_acc[block_rows(b), value_cols[n]] += dv[BLK:]

        each_pair(grad_pass)
        for j, cut in enumerate(heads):
            dq_ref[rows, head_cols(j)] = (dq_acc[:, cut] * score_scale).T.astype(jnp.bfloat16)
        return carry

    lax.fori_loop(0, 2, one, 0)

    def finish(j, carry):
        for n in range(kv_heads):
            key_cols = slice(n * 2 * HD, n * 2 * HD + HD)
            value_cols = slice(n * 2 * HD + HD, (n + 1) * 2 * HD)
            dkv_ref[block_rows(j), key_cols] = (
                dkv_acc[block_rows(j), key_cols] * score_scale
            ).astype(jnp.bfloat16)
            dkv_ref[block_rows(j), value_cols] = dkv_acc[block_rows(j), value_cols].astype(
                jnp.bfloat16
            )
        return carry

    lax.fori_loop(0, block_total, finish, 0)


def attention(lists, counts, order, segments, query, kv, grad_out):
    token_total, kv_width = kv.shape
    block_total = token_total // BLK
    kv_heads = kv_width // (2 * HD)
    head_count = query.shape[1] // HD
    group_size = head_count // kv_heads
    row_total = head_count * BLK
    pair_max = (lists.shape[1] + 1) // 2
    bf16, f32 = jnp.bfloat16, jnp.float32
    smem = pl.BlockSpec(memory_space=pltpu.SMEM)
    vmem = pl.BlockSpec(memory_space=pltpu.VMEM)
    return pl.pallas_call(
        functools.partial(attend, kv_heads, group_size),
        out_shape=(
            jax.ShapeDtypeStruct(query.shape, bf16),
            jax.ShapeDtypeStruct(query.shape, bf16),
            jax.ShapeDtypeStruct(kv.shape, bf16),
        ),
        in_specs=[smem] * 3 + [vmem] * 4,
        out_specs=(vmem,) * 3,
        scratch_shapes=[
            pltpu.SMEM((block_total,), jnp.int32),
            pltpu.VMEM((2 * kv_heads, block_total, HD, BLK), bf16),
            pltpu.VMEM((pair_max, PAIR, row_total), f32),
            pltpu.VMEM((pair_max, PAIR, row_total), bf16),
            pltpu.VMEM((PAIR, row_total), bf16),
            pltpu.VMEM((row_total, HD), bf16),
            pltpu.VMEM((row_total, HD), bf16),
            pltpu.VMEM((HD, row_total), bf16),
            pltpu.VMEM((HD, row_total), f32),
            pltpu.VMEM((HD, row_total), f32),
            pltpu.VMEM((8, row_total), f32),
            pltpu.VMEM((8, row_total), f32),
            pltpu.VMEM((PAIR, BLK), f32),
            pltpu.VMEM((token_total, kv_width), f32),
        ],
        compiler_params=pltpu.CompilerParams(vmem_limit_bytes=56 * 2**20),
        cost_estimate=pl.CostEstimate(
            flops=9 * 10**9, bytes_accessed=10 * 2**20, transcendentals=5 * 10**6
        ),
        name="attend",
    )(lists, counts, order, segments, query, kv, grad_out)


MESH = pl.DeviceIdType.MESH
PIECES = 2
PARTS = 4


def greet(conditions):
    barrier = pltpu.get_barrier_semaphore()
    for present, target in conditions:
        @pl.when(present)
        def _():
            pl.semaphore_signal(barrier, inc=1, device_id=target, device_id_type=MESH)
    pl.semaphore_wait(barrier, sum(present.astype(jnp.int32) for present, _ in conditions))


def line_place(line):
    c = lax.axis_index("ctx")
    z, x = lax.div(c, 2), lax.rem(c, 2)
    return c, z, x, z < line - 1, z > 0


def collect(line, head_count, kv_ref, out_ref, send_sems, recv_sems, local_sem):
    c, z, x, has_up, has_down = line_place(line)
    targets = ({"ctx": c + 2}, {"ctx": c - 2}, {"ctx": c + 1 - 2 * x})
    present = (has_up, has_down, z >= 0)
    shard, width = kv_ref.shape[0], out_ref.shape[1]
    size = shard // PIECES
    first = lax.div(lax.axis_index("head") * head_count, QH // KVH) * 2 * HD
    columns = pl.ds(pl.multiple_of(first, HD), width)
    greet(list(zip(present, targets)))

    def landing(slot, piece):
        return out_ref.at[pl.ds(pl.multiple_of(slot * shard + piece * size, size), size)]

    def copy(slot, piece, way, own=False):
        here = landing(slot, piece)
        source = kv_ref.at[pl.ds(piece * size, size), columns] if own else here
        return pltpu.make_async_remote_copy(
            src_ref=source,
            dst_ref=here,
            send_sem=send_sems.at[slot, piece, way],
            recv_sem=recv_sems.at[slot, piece],
            device_id=targets[way],
            device_id_type=MESH,
        )

    for piece in range(PIECES):
        for way in range(3):
            @pl.when(present[way])
            def _():
                copy(c, piece, way, True).start()
    local = pltpu.make_async_copy(
        kv_ref.at[:, columns],
        out_ref.at[pl.ds(pl.multiple_of(c * shard, shard), shard)],
        local_sem,
    )
    local.start()

    for d in range(1, line):
        for piece in range(PIECES):
            @pl.when(z - d >= 0)
            def _():
                copy(c - 2 * d, piece, 2).wait_recv()

                @pl.when(has_up)
                def _():
                    copy(c - 2 * d, piece, 0).start()

                copy(c - 2 * d, piece, 2).start()

            @pl.when(z + d <= line - 1)
            def _():
                copy(c + 2 * d, piece, 2).wait_recv()

                @pl.when(has_down)
                def _():
                    copy(c + 2 * d, piece, 1).start()

                copy(c + 2 * d, piece, 2).start()

    for other in range(line):
        for piece in range(PIECES):
            copy(2 * other + 1 - x, piece, 2).wait_recv()
            copy(2 * other + x, piece, 2).wait_send()
    for piece in range(PIECES):
        for way in range(2):
            @pl.when(present[way])
            def _():
                copy(c, piece, way, True).wait_send()
    for d in range(1, line):
        for piece in range(PIECES):
            @pl.when((z - d >= 0) & has_up)
            def _():
                copy(c - 2 * d, piece, 0).wait_send()

            @pl.when((z + d <= line - 1) & has_down)
            def _():
                copy(c + 2 * d, piece, 1).wait_send()
    local.wait()


def gather_tokens(keyval, line, head_count, width):
    shard = keyval.shape[0]
    anywhere = pl.BlockSpec(memory_space=pl.ANY)
    return pl.pallas_call(
        functools.partial(collect, line, head_count),
        out_shape=jax.ShapeDtypeStruct((2 * line * shard, width), keyval.dtype),
        in_specs=[anywhere],
        out_specs=anywhere,
        scratch_shapes=[
            pltpu.SemaphoreType.DMA((2 * line, PIECES, 3)),
            pltpu.SemaphoreType.DMA((2 * line, PIECES)),
            pltpu.SemaphoreType.DMA,
        ],
        compiler_params=pltpu.CompilerParams(collective_id=0, has_side_effects=True),
        name="collect",
    )(keyval)


def spread(
    line, exchange, part_ref, out_ref,
    across_buf, up_in, down_in, up_out, down_out,
    across_send, across_recv, up_send, up_recv, down_send, down_recv, head_send, head_recv, own_buf, own_sem,
):
    c, z, x, has_up, has_down = line_place(line)
    shard, width = part_ref.shape[0] // (2 * line), part_ref.shape[1]
    size = shard // PARTS
    f32, bf16 = jnp.float32, jnp.bfloat16
    beside = {"ctx": c + 1 - 2 * x}
    always = z >= 0
    people = [(has_up, {"ctx": c + 2}), (has_down, {"ctx": c - 2}), (always, beside)]
    h = lax.axis_index("head")
    core = lax.rem(h, 2)
    twin, facing = h + 1 - 2 * core, lax.rem(h + 2, 4)
    if exchange:
        people += [(always, {"head": twin}), (always, {"head": facing})]
    greet(people)

    def part_rows(place, piece):
        return pl.ds(pl.multiple_of(place * shard + piece * size, size), size)

    def across(zs, piece):
        return pltpu.make_async_remote_copy(
            src_ref=part_ref.at[part_rows(2 * zs + 1 - x, piece)],
            dst_ref=across_buf.at[zs, piece],
            send_sem=across_send.at[zs, piece],
            recv_sem=across_recv.at[zs, piece],
            device_id=beside,
            device_id_type=MESH,
        )

    def up(zs, piece):
        return pltpu.make_async_remote_copy(
            src_ref=up_out.at[zs, piece],
            dst_ref=up_in.at[zs, piece],
            send_sem=up_send.at[zs, piece],
            recv_sem=up_recv.at[zs, piece],
            device_id={"ctx": c + 2},
            device_id_type=MESH,
        )

    def down(zs, piece):
        return pltpu.make_async_remote_copy(
            src_ref=down_out.at[zs, piece],
            dst_ref=down_in.at[zs, piece],
            send_sem=down_send.at[zs, piece],
            recv_sem=down_recv.at[zs, piece],
            device_id={"ctx": c - 2},
            device_id_type=MESH,
        )

    def to_head(slot, piece, way):
        here = out_ref.at[
            pl.ds(piece * size, size), pl.ds(pl.multiple_of(slot * width, width), width)
        ]
        return pltpu.make_async_remote_copy(
            src_ref=here,
            dst_ref=here,
            send_sem=head_send.at[piece, way],
            recv_sem=head_recv.at[piece, slot],
            device_id={"head": facing if way == 0 else twin},
            device_id_type=MESH,
        )

    lower, upper = z, line - 1 - z
    lone = jnp.abs(upper - lower)

    def place_at(k):
        step = jnp.maximum(k - lone, 0)
        d = jnp.minimum(lower, upper) - lax.div(step, 2)
        paired = jnp.where(lax.rem(step, 2) == 0, z + d, z - d)
        return jnp.where(k < lone, jnp.where(upper > lower, line - 1 - k, k), paired)

    turns = [(k, piece) for piece in range(PARTS) for k in range(line)]
    ahead = 5

    def own_copy(zs):
        rows = pl.ds(pl.multiple_of((2 * zs + x) * shard, shard), shard)
        return pltpu.make_async_copy(part_ref.at[rows], own_buf.at[zs], own_sem.at[zs])

    def launch(turn):
        if turn < len(turns):
            k, piece = turns[turn]
            across(place_at(k), piece).start()

    def add_along(zs, side, piece):
        total = own_buf[zs, pl.ds(piece * size, size), :].astype(f32)
        total = total + across_buf[zs, piece].astype(f32)
        buf, inward, move = (up_out, up_in, up) if side > 0 else (down_out, down_in, down)
        more = has_down if side > 0 else has_up

        @pl.when(more)
        def _():
            move(zs, piece).wait_recv()
            buf[zs, piece] = (total + inward[zs, piece].astype(f32)).astype(bf16)

        @pl.when(jnp.logical_not(more))
        def _():
            buf[zs, piece] = total.astype(bf16)

        move(zs, piece).start()

    def finish(piece):
        rows = pl.ds(piece * size, size)
        total = own_buf[z, rows, :].astype(f32) + across_buf[z, piece].astype(f32)
        if exchange:
            columns = pl.ds(pl.multiple_of(h * width, width), width)
        else:
            columns = slice(None)

        @pl.when(has_down & has_up)
        def _():
            up(z, piece).wait_recv()
            down(z, piece).wait_recv()
            arrived = up_in[z, piece].astype(f32) + down_in[z, piece].astype(f32)
            out_ref[rows, columns] = (total + arrived).astype(bf16)

        @pl.when(has_down & jnp.logical_not(has_up))
        def _():
            up(z, piece).wait_recv()
            out_ref[rows, columns] = (total + up_in[z, piece].astype(f32)).astype(bf16)

        @pl.when(has_up & jnp.logical_not(has_down))
        def _():
            down(z, piece).wait_recv()
            out_ref[rows, columns] = (total + down_in[z, piece].astype(f32)).astype(bf16)

        if exchange:
            to_head(h, piece, 0).start()
            to_head(h, piece, 1).start()

    for turn in range(ahead):
        launch(turn)
    for k in range(line):
        own_copy(place_at(k)).start()
    for turn, (k, piece) in enumerate(turns):
        zs = place_at(k)
        across(zs, piece).wait_recv()
        across(zs, piece).wait_send()
        if piece == 0:
            own_copy(zs).wait()
        launch(turn + ahead)
        if k == line - 1:
            finish(piece)
        else:
            @pl.when(zs > z)
            def _():
                add_along(zs, 1, piece)

            @pl.when(zs < z)
            def _():
                add_along(zs, -1, piece)

    if exchange:
        for piece in range(PARTS):
            to_head(facing, piece, 2).wait_recv()
            to_head(facing, piece, 2).start()
        for piece in range(PARTS):
            to_head(twin, piece, 1).wait_recv()
            to_head(lax.rem(twin + 2, 4), piece, 2).wait_recv()
            to_head(h, piece, 0).wait_send()
            to_head(h, piece, 1).wait_send()
            to_head(facing, piece, 2).wait_send()
    for piece in range(PARTS):
        for zs in range(line):
            @pl.when(zs > z)
            def _():
                up(zs, piece).wait_send()

            @pl.when(zs < z)
            def _():
                down(zs, piece).wait_send()


def reduce_tokens(partial_kv, line, exchange):
    shard, width = partial_kv.shape[0] // (2 * line), partial_kv.shape[1]
    columns = width * (4 if exchange else 1)
    vmem = pl.BlockSpec(memory_space=pltpu.VMEM)
    slots = pltpu.VMEM((line, PARTS, shard // PARTS, width), partial_kv.dtype)
    sems = pltpu.SemaphoreType.DMA((line, PARTS))
    return pl.pallas_call(
        functools.partial(spread, line, exchange),
        out_shape=jax.ShapeDtypeStruct((shard, columns), partial_kv.dtype),
        in_specs=[pl.BlockSpec(memory_space=pl.ANY)],
        out_specs=vmem,
        scratch_shapes=[slots] * 5 + [sems] * 6 + [
            pltpu.SemaphoreType.DMA((PARTS, 3)),
            pltpu.SemaphoreType.DMA((PARTS, 4)),
            pltpu.VMEM((line, shard, width), partial_kv.dtype),
            pltpu.SemaphoreType.DMA((line,)),
        ],
        compiler_params=pltpu.CompilerParams(
            collective_id=1, has_side_effects=True, vmem_limit_bytes=60 * 2**20
        ),
        name="spread",
    )(partial_kv)


def shards(query, keyval, grad_out, vis_blocks, vis_count, segment_ids, block_order):
    head_count = query.shape[1] // HD
    full_group = QH // KVH
    kv_local = max(1, head_count // full_group)
    kv_width = kv_local * 2 * HD
    line = lax.axis_size("ctx") // 2
    exchange = lax.axis_size("head") == 4 and head_count >= full_group
    gathered = gather_tokens(keyval, line, head_count, kv_width)
    attn_out, grad_query, partial_kv = attention(
        vis_blocks, vis_count, block_order, segment_ids.reshape(-1, BLK), query, gathered, grad_out
    )
    summed = reduce_tokens(partial_kv, line, exchange)
    if exchange:
        result = summed.astype(jnp.float32)
    elif head_count >= full_group:
        result = lax.all_gather(summed, "head", axis=1, tiled=True).astype(jnp.float32)
    else:
        first_kv = lax.axis_index("head") * head_count // full_group
        widened = jnp.zeros((summed.shape[0], KVH * 2 * HD), jnp.float32)
        widened = lax.dynamic_update_slice_in_dim(
            widened, summed.astype(jnp.float32), first_kv * 2 * HD, 1
        )
        result = lax.psum(widened.astype(jnp.bfloat16), "head").astype(jnp.float32)
    return (attn_out, grad_query, result)


def solution(mesh):
    placed = (P("ctx", "head"), P("ctx", None), P("ctx", "head"), P(), P(), P(), P())
    return jax.shard_map(
        shards,
        mesh=mesh,
        in_specs=placed,
        out_specs=(P("ctx", "head"), P("ctx", "head"), P("ctx", None)),
        check_vma=False,
    )
```
